512 devices in a mesh: gx: 8 (over z), gy: 8 (over x, core), gz: 8 (over y).
Axes of the slice: x: 4, y: 8, z: 8, core: 2. Of those that a mesh axis runs over, the one named last changes fastest.
Arguments:
- basis: bfloat16 [3584, 64, 4096], P(('gx', 'gy', 'gz')), may hold values from -6 to 6
- density_blocks: bfloat16 [24576, 4096], P(('gx', 'gy', 'gz')), may hold values from -0.014953613 to 0.014953613
- pair_groups: int32 [2, 24576], P(None, ('gx', 'gy', 'gz')), may hold values from 0 to 6, as said below
- owner: int32 [24576, 1], P(('gx', 'gy', 'gz')), may hold values from 0 to 63; in each aligned block of 48 rows (0 to 47, 48 to 95, ...) at most 2 rows name the same one
- owner_slot: int32 [24576], P(('gx', 'gy', 'gz')), may hold values from 0 to 47
Outputs:
- ks_blocks: bfloat16 [24576, 4096], P(('gx', 'gy', 'gz'))
- xc_potential: float32 [64, 64, 64], P('gx', 'gy', 'gz')
The draws below stay inside these ranges and needn't reach their ends.
Inputs may be any that keep to these rules, and one draw needn't show every extreme that they name: At most 2 pairs of one subdomain name the same owner, and in every draw some subdomain's pairs name one owner exactly 2 times; every owner is named by some pair. `pair_groups`: the pairs of one subdomain are distinct ordered pairs of its groups.
All inputs are finite; a program needn't handle non-finite values.
Results may differ from the reference program's by a relative error of at most 0.0055.
Values may be sent and summed in bfloat16 or wider, within the bound.
A program may use at most 64 MiB of HBM per device.

```python
import math
import jax
import jax.numpy as jnp
import numpy as np
from jax import lax

BASIS = 64
GROUPS_DEV = 7
PAIRS_DEV = 48
CELLS = 8
RIM = 4
EXT = 16
EXT3 = 4096
NX = 64
NY = 64
NZ = 64
OWNERS = 64
CAP = 2
BLK_DEV = 48
GROUPS = 3584
PAIRS = 24576
BLOCKS = 24576
N_GX = 8
N_GY = 8
N_GZ = 8


def draw_pair_groups(key, part):
    device_count = PAIRS // PAIRS_DEV
    keys = jax.random.split(jax.random.fold_in(key, 17), device_count)

    def one_device(device_key):
        return jax.random.permutation(device_key, GROUPS_DEV * GROUPS_DEV)[:PAIRS_DEV]
    pair_codes = jax.vmap(one_device)(keys).reshape(-1).astype(jnp.int32)
    return jnp.stack([pair_codes // GROUPS_DEV, pair_codes % GROUPS_DEV]).astype(jnp.int32)


def set_ends(result, rng, smallest, high):
    shape = result.shape
    spot = [jax.random.randint(jax.random.fold_in(rng, axis), (), 0, shape[axis]) for axis in range(len(shape))]
    result = result.at[tuple(spot)].set(smallest)
    longest = shape.index(max(shape))
    spot[longest] = (spot[longest] + 1) % shape[longest]
    return result.at[tuple(spot)].set(high)


def levels(key, shape, pieces, low, high):
    factor_of, own = 1.0, jax.random.fold_in(key, 6)
    for dim, shards_of in pieces:
        heights = jnp.exp(jax.random.uniform(jax.random.fold_in(own, dim), (shards_of,), jnp.float32, low / len(pieces), high / len(pieces)))
        factor_of = factor_of * jnp.repeat(heights, shape[dim] // shards_of).reshape([-1 if axis == dim else 1 for axis in range(len(shape))])
    return factor_of


def routed_block(rng, own, number, rows, number_of, top, most, skew):
    sequence = jax.random.permutation(rng, number_of)
    heavy_load, common = load_shares(number_of, rows * top, most, skew, True), load_shares(number_of, rows * top, most, skew, False)
    places = jnp.arange(number_of)

    def named(sizes, turn):
        used = int((sizes > 0).sum())
        fixed = max(1, used // 4)
        passed = fixed + (places - fixed + turn * (used - fixed)) % max(1, number_of - fixed)
        return jnp.zeros((number_of,), jnp.int32).at[sequence[jnp.where(places < fixed, places, passed)]].set(jnp.asarray(sizes, jnp.int32))

    sizes = jnp.where(number % 4 == 0, named(heavy_load, number // 4), named(common, number - number // 4 - 1))
    mixed = jax.random.permutation(jax.random.fold_in(own, 3), number_of)
    source_of, receiver = mixed[0:number_of // 2 * 2:2], mixed[1:number_of // 2 * 2:2]
    margin = jnp.minimum(sizes[source_of] - 1, most - sizes[receiver]) // 2
    margin = jnp.where((source_of == sequence[0]) | (receiver == sequence[0]) | (sizes[receiver] == 0), 0, jnp.maximum(margin, 0))
    passed = jax.random.randint(jax.random.fold_in(own, 4), (number_of // 2,), 0, 1 << 20) % (margin + 1)
    sizes = sizes.at[source_of].add(-passed).at[receiver].add(passed)
    items = jnp.searchsorted(jnp.cumsum(sizes), jnp.arange(rows * top), side="right").astype(jnp.int32)
    grid = items.reshape(top, rows).T
    grid = grid[jax.random.permutation(jax.random.fold_in(own, 1), rows)]
    turn = jax.random.randint(jax.random.fold_in(own, 2), (rows, 1), 0, top)
    return jnp.take_along_axis(grid, (jnp.arange(top)[None, :] + turn) % top, axis=1)


def load_shares(number_of, total, bound, lean, full):
    portions = [(1 << 20) // math.isqrt(standing ** lean) + 1 for standing in range(1, number_of + 1)]
    largest = bound if full else min(bound, max(-(-total // number_of), total * portions[0] // sum(portions)))
    least = 1 if total - largest >= number_of - 1 else 0
    holding, rest = [largest] + [least] * (number_of - 1), total - largest - least * (number_of - 1)
    while rest > 0:
        movable = [i for i in range(1, number_of) if holding[i] < largest] or [i for i in range(1, number_of) if holding[i] < bound]
        mass, left = sum([portions[i] for i in movable]), rest
        for i in movable:
            extra = min(bound - holding[i], max(1, left * portions[i] // mass), rest)
            holding[i] = holding[i] + extra
            rest = rest - extra
    return np.array(holding)


def noise(rng, dims, deviation, limit, shards=(), kind=jnp.bfloat16):
    entries = jax.random.normal(rng, dims, jnp.float32) * deviation
    if len(shards) > 0:
        entries = levels(rng, dims, shards, -0.22, 0.18) * entries
    return jnp.clip(entries, min=-limit, max=limit).astype(kind)


def setup_inputs(seed: int = 0) -> dict:
    streams_of = jax.random.split(jax.random.key(seed), 6)
    basis = noise(streams_of[0], (GROUPS, BASIS, EXT3), 1.0, 6.0, ((0, 512),))
    density_blocks = noise(streams_of[1], (PAIRS, BASIS * BASIS), 0.0025, 0.014953613, ((0, 512),))
    pair_groups = draw_pair_groups(jax.random.fold_in(streams_of[5], 71), 0)
    owner_keys = jax.random.split(jax.random.fold_in(streams_of[3], 1), PAIRS // PAIRS_DEV)
    owner_turns = jax.random.permutation(jax.random.fold_in(streams_of[3], 3), PAIRS // PAIRS_DEV)
    owner = jax.vmap(lambda own, number: routed_block(jax.random.fold_in(streams_of[3], 2), own, number, PAIRS_DEV, OWNERS, 1, CAP, 2))(owner_keys, owner_turns).reshape((PAIRS, 1))
    owner_slot = set_ends(jax.random.randint(streams_of[4], (PAIRS,), 0, BLK_DEV), jax.random.fold_in(streams_of[4], 1), 0, BLK_DEV - 1).astype(jnp.int32)
    return dict(basis=basis, density_blocks=density_blocks, pair_groups=pair_groups, owner=owner, owner_slot=owner_slot)


XC_COEF = 0.9847450218426965
GRID_WEIGHT = 0.015625


def slater_potential(density):
    return -XC_COEF * density / jnp.cbrt(density * density + 1.0)


def reference(basis, density_blocks, pair_groups, owner, owner_slot):
    devices = N_GX * N_GY * N_GZ
    basis_dev = basis.reshape(devices, GROUPS_DEV, BASIS, EXT3)
    blocks_dev = density_blocks.reshape(devices, PAIRS_DEV, BASIS, BASIS)
    first_group = pair_groups[0].reshape(devices, PAIRS_DEV)
    second_group = pair_groups[1].reshape(devices, PAIRS_DEV)

    def collocate(inputs):
        tables, blocks, left_index, right_index = inputs
        tables32 = tables.astype(jnp.float32)
        right_image = jnp.einsum("pmn,pnr->pmr", blocks.astype(jnp.float32), tables32[right_index])
        return jnp.sum(tables32[left_index] * right_image, axis=(0, 1))

    box_density = lax.map(collocate, (basis_dev, blocks_dev, first_group, second_group))
    device_ids = jnp.arange(devices, dtype=jnp.int32)
    plane_x = device_ids // (N_GY * N_GZ)
    plane_y = (device_ids // N_GZ) % N_GY
    plane_z = device_ids % N_GZ
    offsets = jnp.arange(EXT, dtype=jnp.int32) - RIM
    cell_x = (plane_x[:, None] * CELLS + offsets[None, :]) % NX
    cell_y = (plane_y[:, None] * CELLS + offsets[None, :]) % NY
    cell_z = (plane_z[:, None] * CELLS + offsets[None, :]) % NZ
    flat_cells = (cell_x[:, :, None, None] * (NY * NZ) + cell_y[:, None, :, None] * NZ + cell_z[:, None, None, :]).reshape(devices, EXT3).astype(jnp.int32)
    density = jnp.zeros((NX * NY * NZ,), jnp.float32).at[flat_cells.reshape(-1)].add(box_density.reshape(-1))
    potential = slater_potential(density)
    potential_ext = potential[flat_cells]

    def integrate(inputs):
        tables, local_potential, left_index, right_index = inputs
        tables32 = tables.astype(jnp.float32)
        weighted = (tables32 * local_potential[None, None, :]).astype(jnp.bfloat16)
        weighted = lax.optimization_barrier(weighted).astype(jnp.float32)
        blocks = jnp.einsum("pmr,pnr->pmn", weighted[left_index], tables32[right_index]) * GRID_WEIGHT
        return blocks.astype(jnp.bfloat16).reshape(PAIRS_DEV, BASIS * BASIS)

    pair_blocks = lax.map(integrate, (basis_dev, potential_ext, first_group, second_group))
    owner_dev = owner.reshape(devices, PAIRS_DEV) * N_GZ + plane_z[:, None]
    target_rows = (owner_dev * BLK_DEV + owner_slot.reshape(devices, PAIRS_DEV)).astype(jnp.int32)
    ks_blocks = jnp.zeros((BLOCKS, BASIS * BASIS), jnp.float32).at[target_rows.reshape(-1)].add(pair_blocks.reshape(-1, BASIS * BASIS).astype(jnp.float32))
    return ks_blocks.astype(jnp.bfloat16), potential.reshape(NX, NY, NZ)
```

```python
import functools

import jax
import jax.numpy as jnp
from jax import lax
from jax.experimental import pallas as pl
from jax.experimental.pallas import tpu as pltpu
from jax.sharding import PartitionSpec as P

BASIS = 64
RIM = 4
EXT = 16
EXT3 = 4096
XC_COEF = 0.9847450218426965
GRID_WEIGHT = 0.015625
G = 7
ROWS = G * BASIS
WIDE = 512
N = 8
OWNERS = N * N
PAIRS = 48
CODES = 56
ROW_BLK = 32
MESH = pl.DeviceIdType.MESH
F32 = jnp.float32
BF16 = jnp.bfloat16

CHUNK = 512
NCHUNK = EXT3 // CHUNK

DIRS = [(a, b, c) for c in (0, 1, -1) for a in (0, 1, -1) for b in (0, 1, -1) if (a, b, c) != (0, 0, 0)]
DIR_ID = {d: n for n, d in enumerate(DIRS)}
OUT_PLANE = [d for d in DIRS if d[2] != 0]
PEERS = OWNERS - 1 + len(OUT_PLANE)
FAR_FIRST = (4, 3, 5, 2, 6, 1, 7, 0)


def half(step, low, high, whole):
    return whole if step == 0 else (high if step > 0 else low)


def bytes_wait(ref, sem):
    pltpu.make_async_copy(ref, ref, sem).wait()


def main_kernel(
    sel_ref, basis_ref, blocks_ref, groups_ref, meta_ref,
    recv_ref, mx_ref, pot_ref,
    phi, wgt, a3, mperm, mat, rho, hr, vpot, kb, table, send, mz, xs,
    load_sem, own_sem, halo_send, halo_recv, mz_send, mz_recv, mx_send, mx_recv, blk_send, blk_recv,
):
    i = lax.axis_index("gx")
    j = lax.axis_index("gy")
    k = lax.axis_index("gz")
    me = i * N + j

    loads = []
    for n in range(NCHUNK):
        cols = pl.ds(n * CHUNK, CHUNK)
        copy = pltpu.make_async_copy(basis_ref.at[:, cols], phi.at[:, cols], load_sem.at[n])
        copy.start()
        loads.append(copy)

    barrier = pltpu.get_barrier_semaphore()

    def greet(t, carry):
        pl.semaphore_signal(
            barrier, inc=1,
            device_id=(lax.rem(i + t // N, N), lax.rem(j + lax.rem(t, N), N), k),
            device_id_type=MESH,
        )
        return carry

    lax.fori_loop(1, OWNERS, greet, 0)
    for a, b, c in OUT_PLANE:
        pl.semaphore_signal(
            barrier, inc=1,
            device_id=(lax.rem(i + a + N, N), lax.rem(j + b + N, N), lax.rem(k + c + N, N)),
            device_id_type=MESH,
        )

    lane = lax.broadcasted_iota(jnp.int32, (ROW_BLK, 128), 1)
    low = lane < BASIS
    r64 = lax.broadcasted_iota(jnp.int32, (BASIS, BASIS), 0)
    c64 = lax.broadcasted_iota(jnp.int32, (BASIS, BASIS), 1)
    split_rows = jnp.where(c64 == 2 * (r64 % 32) + r64 // 32, 1.0, 0.0).astype(BF16)
    join_rows = jnp.where(r64 == 2 * (c64 % 32) + c64 // 32, 1.0, 0.0).astype(BF16)

    codes = groups_ref[0:1, :] * G + groups_ref[1:2, :]
    pick = jnp.where(
        lax.broadcasted_iota(jnp.int32, (CODES, PAIRS), 0) == codes, 1.0, 0.0
    ).astype(BF16)
    for n in range(8):
        part = jnp.dot(pick, blocks_ref[:, n * 512:(n + 1) * 512], preferred_element_type=F32)
        for q in range(4):
            a3[pl.ds(n * 4 + q, CODES, stride=ROW_BLK), :] = part[:, q * 128:(q + 1) * 128]
    for a in range(G):
        for bp in range(4):
            even = a3[(a * G + 2 * bp) * ROW_BLK:(a * G + 2 * bp + 1) * ROW_BLK, :]
            if 2 * bp + 1 < G:
                odd = a3[(a * G + 2 * bp + 1) * ROW_BLK:(a * G + 2 * bp + 2) * ROW_BLK, :]
            else:
                odd = jnp.zeros((ROW_BLK, 128), F32)
            top = jnp.where(low, even, pltpu.roll(odd, 64, axis=1))
            bottom = jnp.where(low, pltpu.roll(even, 64, axis=1), odd)
            mperm[a * 64:a * 64 + 32, bp * 128:(bp + 1) * 128] = top.astype(BF16)
            mperm[a * 64 + 32:(a + 1) * 64, bp * 128:(bp + 1) * 128] = bottom.astype(BF16)
        mat[a * 64:(a + 1) * 64, :] = jnp.dot(
            join_rows, mperm[a * 64:(a + 1) * 64, :], preferred_element_type=F32
        ).astype(BF16)

    for n in range(NCHUNK):
        loads[n].wait()
        cols = slice(n * CHUNK, (n + 1) * CHUNK)
        part = phi[:, cols]
        image = jnp.dot(mat[:, :ROWS], part, preferred_element_type=F32)
        line = jnp.sum(part.astype(F32) * image, axis=0, keepdims=True)
        for q in range(CHUNK // 256):
            x = n * (CHUNK // 256) + q
            rho[x:x + 1, :] = line[:, q * 256:(q + 1) * 256]

    pl.semaphore_wait(barrier, PEERS)

    for n, (a, b, c) in enumerate(DIRS):
        src = rho.at[half(a, pl.ds(0, 8), pl.ds(8, 8), pl.ds(0, 16)),
                     half(b, pl.ds(0, 128), pl.ds(128, 128), pl.ds(0, 256))]
        dst = hr.at[n, half(-a, pl.ds(0, 8), pl.ds(8, 8), pl.ds(0, 16)),
                    half(-b, pl.ds(0, 128), pl.ds(128, 128), pl.ds(0, 256))]
        pltpu.make_async_remote_copy(
            src_ref=src, dst_ref=dst, send_sem=halo_send, recv_sem=halo_recv,
            device_id=(lax.rem(i + a + N, N), lax.rem(j + b + N, N), lax.rem(k + c + N, N)),
            device_id_type=MESH,
        ).start()

    def send_z(t, carry):
        ti = lax.rem(i + t, N)
        pltpu.make_async_remote_copy(
            src_ref=meta_ref.at[ti], dst_ref=mz.at[i], send_sem=mz_send, recv_sem=mz_recv,
            device_id=(ti, j, k), device_id_type=MESH,
        ).start()
        return carry

    lax.fori_loop(1, N, send_z, 0)
    mz[i] = meta_ref[i]

    bytes_wait(hr.at[0:11], halo_recv)
    zlow = lax.rem(lax.broadcasted_iota(jnp.int32, (8, 128), 1), EXT) < 8
    for hx in range(2):
        for hy in range(2):
            rows = slice(hx * 8, hx * 8 + 8)
            cols = slice(hy * 128, hy * 128 + 128)
            total = rho[rows, cols]
            steps_x = (0, 1 - 2 * hx)
            steps_y = (0, 1 - 2 * hy)
            for a in steps_x:
                for b in steps_y:
                    if (a, b) != (0, 0):
                        total = total + hr[DIR_ID[(a, b, 0)], rows, cols]
            sides = []
            for c in (1, -1):
                side = None
                for a in steps_x:
                    for b in steps_y:
                        term = hr[DIR_ID[(a, b, c)], rows, cols]
                        side = term if side is None else side + term
                sides.append(side)
            total = total + jnp.where(
                zlow, pltpu.roll(sides[0], 120, axis=1), pltpu.roll(sides[1], 8, axis=1)
            )
            cubic = jnp.exp(jnp.log(total * total + 1.0) * (-1.0 / 3.0))
            vpot[rows, cols] = -XC_COEF * total * cubic
    left = vpot[4:12, 0:128]
    right = vpot[4:12, 128:256]
    lane8 = lax.broadcasted_iota(jnp.int32, (8, 128), 1)
    pot_ref[...] = jnp.where(
        lane8 < 64, pltpu.roll(left, 64, axis=1), pltpu.roll(right, 64, axis=1)
    )

    bytes_wait(mz.at[0:N - 1], mz_recv)
    for t in range(N):
        xs[t] = mz[:, t, :]

    def send_x(t, carry):
        tj = lax.rem(j + t, N)
        pltpu.make_async_remote_copy(
            src_ref=xs.at[tj], dst_ref=mx_ref.at[j], send_sem=mx_send, recv_sem=mx_recv,
            device_id=(i, tj, k), device_id_type=MESH,
        ).start()
        return carry

    lax.fori_loop(1, N, send_x, 0)
    own_meta = pltpu.make_async_copy(xs.at[j], mx_ref.at[j], own_sem.at[0])
    own_meta.start()

    for x in range(EXT):
        cols = slice(x * 256, (x + 1) * 256)
        wgt[:, cols] = (phi[:, cols].astype(F32) * vpot[x:x + 1, :]).astype(BF16)
    ks = lax.dot_general(
        wgt[...], phi[...], (((1,), (1,)), ((), ())), preferred_element_type=F32
    )
    kb[:, 0:ROWS] = (ks * GRID_WEIGHT).astype(BF16)
    kb[:, ROWS:] = jnp.zeros((ROWS, WIDE - ROWS), BF16)
    for a in range(G):
        rows = jnp.dot(split_rows, kb[a * 64:(a + 1) * 64, :], preferred_element_type=F32)
        for bp in range(4):
            top = rows[0:32, bp * 128:(bp + 1) * 128]
            bottom = rows[32:64, bp * 128:(bp + 1) * 128]
            table[a * G + 2 * bp] = jnp.where(low, top, pltpu.roll(bottom, 64, axis=1)).astype(BF16)
            if 2 * bp + 1 < G:
                table[a * G + 2 * bp + 1] = jnp.where(
                    low, pltpu.roll(top, 64, axis=1), bottom
                ).astype(BF16)

    def pack(target):
        send[target, 0] = table[sel_ref[target]]
        send[target, 1] = table[sel_ref[OWNERS + target]]

    for di in FAR_FIRST:
        ti = lax.rem(i + di, N)

        def send_block(t, carry, ti=ti):
            tj = lax.rem(j + t, N)
            target = ti * N + tj
            pack(target)
            pltpu.make_async_remote_copy(
                src_ref=send.at[target], dst_ref=recv_ref.at[me], send_sem=blk_send,
                recv_sem=blk_recv, device_id=(ti, tj, k), device_id_type=MESH,
            ).start()
            return carry

        lax.fori_loop(0 if di else 1, N, send_block, 0)
    pack(me)
    own = pltpu.make_async_copy(send.at[me], recv_ref.at[me], own_sem.at[1])
    own.start()

    own.wait()
    own_meta.wait()
    bytes_wait(xs.at[0:N - 1], mx_send)
    bytes_wait(mz.at[0:N - 1], mz_send)
    bytes_wait(hr.at[0:11], halo_send)
    bytes_wait(mx_ref.at[0:N - 1], mx_recv)
    bytes_wait(send.at[0:OWNERS - 1], blk_send)
    bytes_wait(recv_ref.at[0:OWNERS - 1], blk_recv)


def store_kernel(mx_ref, recv_ref, out_ref, acc):
    acc[...] = jnp.zeros_like(acc)

    def add(t, carry):
        row = (t % N) * N + t // N
        for rank in range(2):
            slot = mx_ref[row, rank * 64]
            slot = jnp.where(slot < 0, PAIRS, slot)
            at = pl.ds(pl.multiple_of(slot * ROW_BLK, ROW_BLK), ROW_BLK)
            acc[at, :] += recv_ref[t, rank].astype(F32)
        return carry

    lax.fori_loop(0, OWNERS, add, 0)
    for c in range(ROW_BLK):
        out_ref[:, c * 128:(c + 1) * 128] = acc[pl.ds(c, PAIRS, stride=ROW_BLK), :].astype(BF16)


def per_device(basis, density_blocks, pair_groups, owner, owner_slot):
    codes = pair_groups[0] * G + pair_groups[1]
    names = owner[:, 0]
    order = jnp.arange(PAIRS, dtype=jnp.int32)
    earlier = (names[:, None] == names[None, :]) & (order[:, None] > order[None, :])
    rank = jnp.sum(earlier.astype(jnp.int32), axis=1)
    place = rank * OWNERS + names
    match = jnp.arange(2 * OWNERS, dtype=jnp.int32)[:, None] == place[None, :]
    sel = jnp.sum(jnp.where(match, codes[None, :], 0), axis=1)
    slots = jnp.sum(jnp.where(match, owner_slot[None, :] + 1, 0), axis=1) - 1
    meta = jnp.broadcast_to(slots.reshape(2, N, N, 1), (2, N, N, 64))
    meta = jnp.concatenate([meta[0], meta[1]], axis=-1)

    vmem = pl.BlockSpec(memory_space=pltpu.VMEM)
    smem = pl.BlockSpec(memory_space=pltpu.SMEM)
    hbm = pl.BlockSpec(memory_space=pl.ANY)
    recv, mx, pot = pl.pallas_call(
        main_kernel,
        name="collocate_exchange",
        out_shape=(
            jax.ShapeDtypeStruct((OWNERS, 2, ROW_BLK, 128), BF16),
            jax.ShapeDtypeStruct((N, N, 128), jnp.int32),
            jax.ShapeDtypeStruct((8, 128), F32),
        ),
        in_specs=[smem, hbm, vmem, vmem, vmem],
        out_specs=(hbm, hbm, vmem),
        scratch_shapes=[
            pltpu.VMEM((ROWS, EXT3), BF16),
            pltpu.VMEM((ROWS, EXT3), BF16),
            pltpu.VMEM((CODES * ROW_BLK, 128), F32),
            pltpu.VMEM((ROWS, WIDE), BF16),
            pltpu.VMEM((ROWS, WIDE), BF16),
            pltpu.VMEM((EXT, 256), F32),
            pltpu.VMEM((len(DIRS), EXT, 256), F32),
            pltpu.VMEM((EXT, 256), F32),
            pltpu.VMEM((ROWS, WIDE), BF16),
            pltpu.VMEM((G * G, ROW_BLK, 128), BF16),
            pltpu.VMEM((OWNERS, 2, ROW_BLK, 128), BF16),
            pltpu.VMEM((N, N, 128), jnp.int32),
            pltpu.VMEM((N, N, 128), jnp.int32),
            pltpu.SemaphoreType.DMA((NCHUNK,)),
            pltpu.SemaphoreType.DMA((2,)),
        ] + [pltpu.SemaphoreType.DMA] * 8,
        compiler_params=pltpu.CompilerParams(
            collective_id=1, has_side_effects=True, vmem_limit_bytes=40 << 20
        ),
        cost_estimate=pl.CostEstimate(
            flops=4 * ROWS * ROWS * EXT3, bytes_accessed=6 << 20, transcendentals=2 * EXT3
        ),
    )(sel, basis.reshape(ROWS, EXT3), density_blocks, pair_groups, meta)

    ks_blocks = pl.pallas_call(
        store_kernel,
        name="store_blocks",
        out_shape=jax.ShapeDtypeStruct((PAIRS, 4096), BF16),
        in_specs=[smem, vmem],
        out_specs=vmem,
        scratch_shapes=[pltpu.VMEM(((PAIRS + 1) * ROW_BLK, 128), F32)],
        compiler_params=pltpu.CompilerParams(vmem_limit_bytes=32 << 20),
    )(mx.reshape(N * N, 128), recv)
    potential = pot.reshape(8, 8, EXT)[:, :, RIM:RIM + 8]
    return ks_blocks, potential


def solution(mesh):
    return jax.shard_map(
        per_device,
        mesh=mesh,
        in_specs=(
            P(("gx", "gy", "gz"), None, None),
            P(("gx", "gy", "gz"), None),
            P(None, ("gx", "gy", "gz")),
            P(("gx", "gy", "gz"), None),
            P(("gx", "gy", "gz")),
        ),
        out_specs=(P(("gx", "gy", "gz"), None), P("gx", "gy", "gz")),
        check_vma=False,
    )
```

```python
import functools

import jax
import jax.numpy as jnp
from jax import lax
from jax.experimental import pallas as pl
from jax.experimental.pallas import tpu as pltpu
from jax.sharding import PartitionSpec as P

BASIS = 64
RIM = 4
EXT = 16
EXT3 = 4096
XC_COEF = 0.9847450218426965
GRID_WEIGHT = 0.015625
G = 7
ROWS = G * BASIS
WIDE = 512
N = 8
OWNERS = N * N
PAIRS = 48
CODES = 56
ROW_BLK = 32
MESH = pl.DeviceIdType.MESH
F32 = jnp.float32
BF16 = jnp.bfloat16

CHUNK = 512
NCHUNK = EXT3 // CHUNK

DIRS = [(a, b, c) for c in (0, 1, -1) for a in (0, 1, -1) for b in (0, 1, -1) if (a, b, c) != (0, 0, 0)]
DIR_ID = {d: n for n, d in enumerate(DIRS)}
OUT_PLANE = [d for d in DIRS if d[2] != 0]
FAR_Z = (2, 3, 4, 5, 6)
PEERS = OWNERS - 1 + len(OUT_PLANE) + len(FAR_Z)
FAR_FIRST = (4, 3, 5, 2, 6, 1, 7, 0)
SECOND = 3
PARTS = 4
FLAG = 128


def half(step, low, high, whole):
    return whole if step == 0 else (high if step > 0 else low)


def bytes_wait(ref, sem):
    pltpu.make_async_copy(ref, ref, sem).wait()


def main_kernel(
    basis_ref, blocks_ref, groups_ref, owner_ref, slot_ref,
    recv_ref, recv2_ref, slots_out, flag_out, pot_ref, table_ref,
    phi, wgt, blk, gv, ov, sv, a3, mperm, mat, rho, hr, vpot, kb, table, send, z2s, z2r, x2s,
    selv, sels, meta, mz, xs, mx, fl, fr, potv, slotv,
    load_sem, own_sem, halo_send, halo_recv, mz_send, mz_recv, mx_send, mx_recv, blk_send, blk_recv,
    z2_send, z2_recv, x2_send, x2_recv, fl_send, fl_recv,
):
    i = lax.axis_index("gx")
    j = lax.axis_index("gy")
    k = lax.axis_index("gz")
    me = i * N + j

    small = []
    for n, (src, dst) in enumerate(((groups_ref, gv), (owner_ref, ov), (slot_ref, sv), (blocks_ref, blk))):
        copy = pltpu.make_async_copy(src, dst, load_sem.at[NCHUNK + n])
        copy.start()
        small.append(copy)
    loads = []
    for n in range(NCHUNK):
        cols = pl.ds(n * CHUNK, CHUNK)
        copy = pltpu.make_async_copy(basis_ref.at[:, cols], phi.at[:, cols], load_sem.at[n])
        copy.start()
        loads.append(copy)

    barrier = pltpu.get_barrier_semaphore()

    def greet(t, carry):
        pl.semaphore_signal(
            barrier, inc=1,
            device_id=(lax.rem(i + t // N, N), lax.rem(j + lax.rem(t, N), N), k),
            device_id_type=MESH,
        )
        return carry

    lax.fori_loop(1, OWNERS, greet, 0)
    for a, b, c in OUT_PLANE + [(0, 0, t) for t in FAR_Z]:
        pl.semaphore_signal(
            barrier, inc=1,
            device_id=(lax.rem(i + a + N, N), lax.rem(j + b + N, N), lax.rem(k + c + N, N)),
            device_id_type=MESH,
        )

    lane = lax.broadcasted_iota(jnp.int32, (ROW_BLK, 128), 1)
    low = lane < BASIS
    r64 = lax.broadcasted_iota(jnp.int32, (BASIS, BASIS), 0)
    c64 = lax.broadcasted_iota(jnp.int32, (BASIS, BASIS), 1)
    split_rows = jnp.where(c64 == 2 * (r64 % 32) + r64 // 32, 1.0, 0.0).astype(BF16)
    join_rows = jnp.where(r64 == 2 * (c64 % 32) + c64 // 32, 1.0, 0.0).astype(BF16)

    for copy in small[:3]:
        copy.wait()
    row = lax.broadcasted_iota(jnp.int32, (PAIRS, PAIRS), 0)
    col = lax.broadcasted_iota(jnp.int32, (PAIRS, PAIRS), 1)

    def upright(line):
        return jnp.sum(jnp.where(row == col, line, 0), axis=1, keepdims=True)

    def count(mask, axis):
        return jnp.sum(jnp.where(mask, 1, 0), axis=axis, keepdims=True)

    codes = gv[0:1, :] * G + gv[1:2, :]
    own_r = ov[...]
    own_c = upright(own_r)
    code_c = upright(codes)
    grp_r = own_r // N
    grp_c = own_c // N
    same = own_c == own_r
    rank_c = count(same & (col < row), 1)
    rank_r = count(same & (row < col), 0)
    mates = grp_c == grp_r
    idx_c = count(mates & (own_r < own_c) & (rank_r > 0), 1)
    idx_r = count(mates & (own_c < own_r) & (rank_c > 0), 0)
    place_c = rank_c * OWNERS + own_c
    place_r = rank_r * OWNERS + own_r
    wide = lax.broadcasted_iota(jnp.int32, (PAIRS, 128), 1)
    sel1 = jnp.sum(jnp.where(wide == place_c, code_c, 0), axis=0, keepdims=True)
    second_at = jnp.where((rank_c > 0) & (idx_c < SECOND), grp_c * SECOND + idx_c, -1)
    sel2 = jnp.sum(jnp.where(wide == second_at, code_c, 0), axis=0, keepdims=True)
    selv[0:1, :] = sel1
    selv[1:2, :] = sel2
    sel_copy = pltpu.make_async_copy(selv, sels, own_sem.at[0])
    sel_copy.start()
    tall = lax.broadcasted_iota(jnp.int32, (OWNERS, PAIRS), 0)
    first_m = tall == place_r
    second_m = tall + OWNERS == place_r
    first_slot = jnp.sum(jnp.where(first_m, sv[...] + 1, 0), axis=1, keepdims=True) - 1
    second_slot = jnp.sum(jnp.where(second_m, sv[...] + 1, 0), axis=1, keepdims=True) - 1
    second_idx = jnp.sum(jnp.where(second_m, idx_r + 1, 0), axis=1, keepdims=True) - 1
    over = jnp.max(jnp.where((rank_r > 0) & (idx_r >= SECOND), FLAG, 0), axis=1, keepdims=True)
    wide64 = lax.broadcasted_iota(jnp.int32, (OWNERS, 128), 1)
    tile = jnp.where(wide64 < OWNERS, first_slot + over, second_slot)
    index = jnp.broadcast_to(second_idx, (OWNERS, 128))
    for t in range(N):
        meta[t, 0] = tile[t * N:(t + 1) * N]
        meta[t, 1] = index[t * N:(t + 1) * N]

    pick = jnp.where(
        lax.broadcasted_iota(jnp.int32, (CODES, PAIRS), 0) == codes, 1.0, 0.0
    ).astype(BF16)
    small[3].wait()
    for n in range(8):
        part = jnp.dot(pick, blk[:, n * 512:(n + 1) * 512], preferred_element_type=F32)
        for q in range(4):
            a3[pl.ds(n * 4 + q, CODES, stride=ROW_BLK), :] = part[:, q * 128:(q + 1) * 128]
    for a in range(G):
        for bp in range(4):
            even = a3[(a * G + 2 * bp) * ROW_BLK:(a * G + 2 * bp + 1) * ROW_BLK, :]
            if 2 * bp + 1 < G:
                odd = a3[(a * G + 2 * bp + 1) * ROW_BLK:(a * G + 2 * bp + 2) * ROW_BLK, :]
            else:
                odd = jnp.zeros((ROW_BLK, 128), F32)
            top = jnp.where(low, even, pltpu.roll(odd, 64, axis=1))
            bottom = jnp.where(low, pltpu.roll(even, 64, axis=1), odd)
            mperm[a * 64:a * 64 + 32, bp * 128:(bp + 1) * 128] = top.astype(BF16)
            mperm[a * 64 + 32:(a + 1) * 64, bp * 128:(bp + 1) * 128] = bottom.astype(BF16)
        mat[a * 64:(a + 1) * 64, :] = jnp.dot(
            join_rows, mperm[a * 64:(a + 1) * 64, :], preferred_element_type=F32
        ).astype(BF16)

    for n in range(NCHUNK):
        loads[n].wait()
        cols = slice(n * CHUNK, (n + 1) * CHUNK)
        part = phi[:, cols]
        image = jnp.dot(mat[:, :ROWS], part, preferred_element_type=F32)
        line = jnp.sum(part.astype(F32) * image, axis=0, keepdims=True)
        for q in range(CHUNK // 256):
            x = n * (CHUNK // 256) + q
            rho[x:x + 1, :] = line[:, q * 256:(q + 1) * 256]

    pl.semaphore_wait(barrier, PEERS)

    for n, (a, b, c) in enumerate(DIRS):
        src = rho.at[half(a, pl.ds(0, 8), pl.ds(8, 8), pl.ds(0, 16)),
                     half(b, pl.ds(0, 128), pl.ds(128, 128), pl.ds(0, 256))]
        dst = hr.at[n, half(-a, pl.ds(0, 8), pl.ds(8, 8), pl.ds(0, 16)),
                    half(-b, pl.ds(0, 128), pl.ds(128, 128), pl.ds(0, 256))]
        pltpu.make_async_remote_copy(
            src_ref=src, dst_ref=dst, send_sem=halo_send, recv_sem=halo_recv,
            device_id=(lax.rem(i + a + N, N), lax.rem(j + b + N, N), lax.rem(k + c + N, N)),
            device_id_type=MESH,
        ).start()

    def send_z(t, carry):
        ti = lax.rem(i + t, N)
        pltpu.make_async_remote_copy(
            src_ref=meta.at[ti], dst_ref=mz.at[i], send_sem=mz_send, recv_sem=mz_recv,
            device_id=(ti, j, k), device_id_type=MESH,
        ).start()
        return carry

    lax.fori_loop(1, N, send_z, 0)
    mz[i] = meta[i]

    bytes_wait(hr.at[0:11], halo_recv)
    zlow = lax.rem(lax.broadcasted_iota(jnp.int32, (8, 128), 1), EXT) < 8
    for hx in range(2):
        for hy in range(2):
            rows = slice(hx * 8, hx * 8 + 8)
            cols = slice(hy * 128, hy * 128 + 128)
            total = rho[rows, cols]
            steps_x = (0, 1 - 2 * hx)
            steps_y = (0, 1 - 2 * hy)
            for a in steps_x:
                for b in steps_y:
                    if (a, b) != (0, 0):
                        total = total + hr[DIR_ID[(a, b, 0)], rows, cols]
            sides = []
            for c in (1, -1):
                side = None
                for a in steps_x:
                    for b in steps_y:
                        term = hr[DIR_ID[(a, b, c)], rows, cols]
                        side = term if side is None else side + term
                sides.append(side)
            total = total + jnp.where(
                zlow, pltpu.roll(sides[0], 120, axis=1), pltpu.roll(sides[1], 8, axis=1)
            )
            cubic = jnp.exp(jnp.log(total * total + 1.0) * (-1.0 / 3.0))
            vpot[rows, cols] = -XC_COEF * total * cubic
    left = vpot[4:12, 0:128]
    right = vpot[4:12, 128:256]
    lane8 = lax.broadcasted_iota(jnp.int32, (8, 128), 1)
    potv[...] = jnp.where(
        lane8 < 64, pltpu.roll(left, 64, axis=1), pltpu.roll(right, 64, axis=1)
    )
    pot_copy = pltpu.make_async_copy(potv, pot_ref, own_sem.at[3])
    pot_copy.start()

    bytes_wait(mz.at[0:N - 1], mz_recv)
    for t in range(N):
        xs[t] = mz[:, 0, t, :]

    def send_x(t, carry):
        tj = lax.rem(j + t, N)
        pltpu.make_async_remote_copy(
            src_ref=xs.at[tj], dst_ref=mx.at[j], send_sem=mx_send, recv_sem=mx_recv,
            device_id=(i, tj, k), device_id_type=MESH,
        ).start()
        return carry

    lax.fori_loop(1, N, send_x, 0)
    mx[j] = xs[j]

    for x in range(EXT):
        cols = slice(x * 256, (x + 1) * 256)
        wgt[:, cols] = (phi[:, cols].astype(F32) * vpot[x:x + 1, :]).astype(BF16)
    ks = lax.dot_general(
        wgt[...], phi[...], (((1,), (1,)), ((), ())), preferred_element_type=F32
    )
    kb[:, 0:ROWS] = (ks * GRID_WEIGHT).astype(BF16)
    kb[:, ROWS:] = jnp.zeros((ROWS, WIDE - ROWS), BF16)
    for a in range(G):
        rows = jnp.dot(split_rows, kb[a * 64:(a + 1) * 64, :], preferred_element_type=F32)
        for bp in range(4):
            top = rows[0:32, bp * 128:(bp + 1) * 128]
            bottom = rows[32:64, bp * 128:(bp + 1) * 128]
            table[a * G + 2 * bp] = jnp.where(low, top, pltpu.roll(bottom, 64, axis=1)).astype(BF16)
            if 2 * bp + 1 < G:
                table[a * G + 2 * bp + 1] = jnp.where(
                    low, pltpu.roll(top, 64, axis=1), bottom
                ).astype(BF16)

    sel_copy.wait()
    keep = pltpu.make_async_copy(table, table_ref, own_sem.at[0])
    keep.start()

    def pack_second(t, carry):
        for c in range(SECOND):
            z2s[t, c] = table[sels[1, t * SECOND + c]]
        return carry

    lax.fori_loop(0, N, pack_second, 0)

    def send_second(t, carry):
        ti = lax.rem(i + t, N)
        pltpu.make_async_remote_copy(
            src_ref=z2s.at[ti], dst_ref=z2r.at[i], send_sem=z2_send, recv_sem=z2_recv,
            device_id=(ti, j, k), device_id_type=MESH,
        ).start()
        return carry

    lax.fori_loop(1, N, send_second, 0)
    z2r[i] = z2s[i]

    for di in FAR_FIRST:
        ti = lax.rem(i + di, N)

        def send_block(t, carry, ti=ti):
            tj = lax.rem(j + t, N)
            target = ti * N + tj
            send[target] = table[sels[0, target]]
            pltpu.make_async_remote_copy(
                src_ref=send.at[target], dst_ref=recv_ref.at[me], send_sem=blk_send,
                recv_sem=blk_recv, device_id=(ti, tj, k), device_id_type=MESH,
            ).start()
            return carry

        lax.fori_loop(0 if di else 1, N, send_block, 0)
    send[me] = table[sels[0, me]]
    own = pltpu.make_async_copy(send.at[me], recv_ref.at[me], own_sem.at[1])
    own.start()

    bytes_wait(mx.at[0:N - 1], mx_recv)
    wide8 = lax.broadcasted_iota(jnp.int32, (N, 128), 1)
    sub8 = lax.broadcasted_iota(jnp.int32, (N, 128), 0)
    slots = jnp.zeros((N, 128), jnp.int32)
    over = jnp.zeros((N, 128), jnp.int32)
    for t in range(N):
        part = mx[t]
        left_over = (wide8 < OWNERS) & (part >= FLAG - 1)
        over = jnp.maximum(over, jnp.where(left_over, 1, 0))
        value = jnp.where(left_over, part - FLAG, part)
        here = (wide8 == sub8 * N + t) | (wide8 == OWNERS + t * N + sub8)
        slots = slots + jnp.where(here, value, 0)
    slotv[...] = jnp.broadcast_to(jnp.sum(slots, axis=0, keepdims=True), (N, 128))
    slot_copy = pltpu.make_async_copy(slotv, slots_out, own_sem.at[4])
    slot_copy.start()
    fl[...] = over

    def send_flag(t, carry):
        tk = lax.rem(k + t, N)
        pltpu.make_async_remote_copy(
            src_ref=fl, dst_ref=fr.at[k], send_sem=fl_send, recv_sem=fl_recv,
            device_id=(i, j, tk), device_id_type=MESH,
        ).start()
        return carry

    lax.fori_loop(1, N, send_flag, 0)
    fr[k] = over

    bytes_wait(z2r.at[0:N - 1], z2_recv)
    for t in range(N):
        def place_second(a, carry, t=t):
            index = jnp.broadcast_to(mz[a, 1, t:t + 1, :], (ROW_BLK, 128))
            total = jnp.zeros((ROW_BLK, 128), F32)
            for c in range(SECOND):
                total = jnp.where(index == c, z2r[a, c].astype(F32), total)
            x2s[t, a] = total.astype(BF16)
            return carry

        lax.fori_loop(0, N, place_second, 0)

    def forward(t, carry):
        tj = lax.rem(j + t, N)
        pltpu.make_async_remote_copy(
            src_ref=x2s.at[tj], dst_ref=recv2_ref.at[j], send_sem=x2_send, recv_sem=x2_recv,
            device_id=(i, tj, k), device_id_type=MESH,
        ).start()
        return carry

    lax.fori_loop(1, N, forward, 0)
    own2 = pltpu.make_async_copy(x2s.at[j], recv2_ref.at[j], own_sem.at[2])
    own2.start()

    bytes_wait(fr.at[0:N - 1], fl_recv)
    for t in range(N):
        over = jnp.maximum(over, fr[t])
    flag_out[...] = jnp.max(jnp.max(over, axis=0, keepdims=True), axis=1, keepdims=True)

    for copy in (keep, pot_copy, slot_copy):
        copy.wait()
    own.wait()
    own2.wait()
    bytes_wait(fr.at[0:N - 1], fl_send)
    bytes_wait(xs.at[0:N - 1], mx_send)
    bytes_wait(mz.at[0:N - 1], mz_send)
    bytes_wait(hr.at[0:11], halo_send)
    bytes_wait(z2s.at[0:N - 1], z2_send)
    bytes_wait(x2s.at[0:N - 1], x2_send)
    bytes_wait(send.at[0:OWNERS - 1], blk_send)
    bytes_wait(recv2_ref.at[0:N - 1], x2_recv)
    bytes_wait(recv_ref.at[0:OWNERS - 1], blk_recv)


def store_kernel(
    slots_ref, recv_ref, recv2_ref, pot_ref, out_ref, pot_out,
    acc, slots, got, got2, pot, cells, rows, sem, out_sem,
):
    def start(src, dst, at):
        copy = pltpu.make_async_copy(src, dst, at)
        copy.start()
        return copy

    few = OWNERS // PARTS
    slots_in = start(slots_ref, slots, sem.at[2 * PARTS])
    pot_in = start(pot_ref, pot, sem.at[2 * PARTS + 1])
    parts = []
    for n in range(PARTS):
        part = pl.ds(n * few, few)
        parts.append((
            start(recv_ref.at[part], got.at[part], sem.at[2 * n]),
            start(recv2_ref.at[part], got2.at[part], sem.at[2 * n + 1]),
        ))
    acc[...] = jnp.zeros_like(acc)
    pot_in.wait()
    for y in range(8):
        cells[:, y, :] = pot[:, y * EXT + RIM:y * EXT + RIM + 8]
    outs = [start(cells, pot_out, out_sem.at[PARTS])]

    def add(t, carry):
        for rank, ref in enumerate((got, got2)):
            slot = slots[0, rank * OWNERS + t]
            slot = jnp.where(slot < 0, PAIRS, slot)
            at = pl.ds(pl.multiple_of(slot * ROW_BLK, ROW_BLK), ROW_BLK)
            acc[at, :] += ref[t].astype(F32)
        return carry

    slots_in.wait()
    for n in range(PARTS):
        for copy in parts[n]:
            copy.wait()
        lax.fori_loop(n * few, (n + 1) * few, add, 0, unroll=4)
    wide = ROW_BLK // PARTS
    for n in range(PARTS):
        for c in range(n * wide, (n + 1) * wide):
            rows[:, c * 128:(c + 1) * 128] = acc[pl.ds(c, PAIRS, stride=ROW_BLK), :].astype(BF16)
        cols = pl.ds(n * wide * 128, wide * 128)
        outs.append(start(rows.at[:, cols], out_ref.at[:, cols], out_sem.at[n]))
    for copy in outs:
        copy.wait()


def store(slots, recv, recv2, pot):
    hbm = pl.BlockSpec(memory_space=pl.ANY)
    return pl.pallas_call(
        store_kernel,
        name="store_blocks",
        out_shape=(
            jax.ShapeDtypeStruct((PAIRS, 4096), BF16),
            jax.ShapeDtypeStruct((8, 8, 8), F32),
        ),
        in_specs=[hbm] * 4,
        out_specs=(hbm, hbm),
        scratch_shapes=[
            pltpu.VMEM(((PAIRS + 1) * ROW_BLK, 128), F32),
            pltpu.SMEM((8, 128), jnp.int32),
            pltpu.VMEM((OWNERS, ROW_BLK, 128), BF16),
            pltpu.VMEM((OWNERS, ROW_BLK, 128), BF16),
            pltpu.VMEM((8, 128), F32),
            pltpu.VMEM((8, 8, 8), F32),
            pltpu.VMEM((PAIRS, 4096), BF16),
            pltpu.SemaphoreType.DMA((2 * PARTS + 2,)),
            pltpu.SemaphoreType.DMA((PARTS + 1,)),
        ],
        compiler_params=pltpu.CompilerParams(vmem_limit_bytes=61 << 20),
    )(slots, recv, recv2, pot)


def resend(pair_groups, owner, owner_slot, table, slots, recv, recv2, pot):
    codes = pair_groups[0] * G + pair_groups[1]
    names = owner[:, 0]
    order = jnp.arange(PAIRS, dtype=jnp.int32)
    earlier = (names[:, None] == names[None, :]) & (order[:, None] > order[None, :])
    rank = jnp.sum(earlier.astype(jnp.int32), axis=1)
    match = (jnp.arange(OWNERS, dtype=jnp.int32)[:, None] == names[None, :]) & (rank[None, :] == 1)
    pick = jnp.sum(jnp.where(match, codes[None, :], 0), axis=1)
    second = jnp.sum(jnp.where(match, owner_slot[None, :] + 1, 0), axis=1) - 1
    chosen = (jnp.arange(G * G, dtype=jnp.int32)[None, :] == pick[:, None]).astype(BF16)
    blocks = lax.dot_general(
        chosen, table, (((1,), (0,)), ((), ())), preferred_element_type=F32
    ).astype(BF16)
    got = lax.all_to_all(blocks, ("gx", "gy"), split_axis=0, concat_axis=0, tiled=True)
    got_slots = lax.all_to_all(second, ("gx", "gy"), split_axis=0, concat_axis=0, tiled=True)
    new = jnp.concatenate([slots[:, :OWNERS], jnp.broadcast_to(got_slots[None], (N, OWNERS))], axis=1)
    return store(new, recv, got, pot)


def per_device(basis, density_blocks, pair_groups, owner, owner_slot):
    vmem = pl.BlockSpec(memory_space=pltpu.VMEM)
    hbm = pl.BlockSpec(memory_space=pl.ANY)
    block = (ROW_BLK, 128)
    dma = pltpu.SemaphoreType.DMA
    recv, recv2, slots, flag, pot, table = pl.pallas_call(
        main_kernel,
        name="collocate_exchange",
        out_shape=(
            jax.ShapeDtypeStruct((OWNERS, *block), BF16),
            jax.ShapeDtypeStruct((N, N, *block), BF16),
            jax.ShapeDtypeStruct((N, 128), jnp.int32),
            jax.ShapeDtypeStruct((1, 1), jnp.int32),
            jax.ShapeDtypeStruct((8, 128), F32),
            jax.ShapeDtypeStruct((G * G, *block), BF16),
        ),
        in_specs=[hbm] * 5,
        out_specs=(hbm, hbm, hbm, vmem, hbm, hbm),
        scratch_shapes=[
            pltpu.VMEM((ROWS, EXT3), BF16),
            pltpu.VMEM((ROWS, EXT3), BF16),
            pltpu.VMEM((PAIRS, 4096), BF16),
            pltpu.VMEM((2, PAIRS), jnp.int32),
            pltpu.VMEM((1, PAIRS), jnp.int32),
            pltpu.VMEM((1, PAIRS), jnp.int32),
            pltpu.VMEM((CODES * ROW_BLK, 128), F32),
            pltpu.VMEM((ROWS, WIDE), BF16),
            pltpu.VMEM((ROWS, WIDE), BF16),
            pltpu.VMEM((EXT, 256), F32),
            pltpu.VMEM((len(DIRS), EXT, 256), F32),
            pltpu.VMEM((EXT, 256), F32),
            pltpu.VMEM((ROWS, WIDE), BF16),
            pltpu.VMEM((G * G, *block), BF16),
            pltpu.VMEM((OWNERS, *block), BF16),
            pltpu.VMEM((N, SECOND, *block), BF16),
            pltpu.VMEM((N, SECOND, *block), BF16),
            pltpu.VMEM((N, N, *block), BF16),
            pltpu.VMEM((2, 128), jnp.int32),
            pltpu.SMEM((2, 128), jnp.int32),
            pltpu.VMEM((N, 2, N, 128), jnp.int32),
            pltpu.VMEM((N, 2, N, 128), jnp.int32),
            pltpu.VMEM((N, N, 128), jnp.int32),
            pltpu.VMEM((N, N, 128), jnp.int32),
            pltpu.VMEM((N, 128), jnp.int32),
            pltpu.VMEM((N, N, 128), jnp.int32),
            pltpu.VMEM((8, 128), F32),
            pltpu.VMEM((N, 128), jnp.int32),
            dma((NCHUNK + 4,)),
            dma((5,)),
        ] + [dma] * 14,
        compiler_params=pltpu.CompilerParams(
            collective_id=1, has_side_effects=True, vmem_limit_bytes=61 << 20
        ),
        cost_estimate=pl.CostEstimate(
            flops=4 * ROWS * ROWS * EXT3, bytes_accessed=6 << 20, transcendentals=2 * EXT3
        ),
    )(
        basis.reshape(ROWS, EXT3), density_blocks, pair_groups,
        owner.reshape(1, PAIRS), owner_slot.reshape(1, PAIRS),
    )
    recv2 = recv2.reshape(OWNERS, *block)
    return lax.cond(
        flag[0, 0] > 0,
        lambda: resend(pair_groups, owner, owner_slot, table, slots, recv, recv2, pot),
        lambda: store(slots, recv, recv2, pot),
    )


def solution(mesh):
    return jax.shard_map(
        per_device,
        mesh=mesh,
        in_specs=(
            P(("gx", "gy", "gz"), None, None),
            P(("gx", "gy", "gz"), None),
            P(None, ("gx", "gy", "gz")),
            P(("gx", "gy", "gz"), None),
            P(("gx", "gy", "gz")),
        ),
        out_specs=(P(("gx", "gy", "gz"), None), P("gx", "gy", "gz")),
        check_vma=False,
    )
```

```python
import functools

import jax
import jax.numpy as jnp
from jax import lax
from jax.experimental import pallas as pl
from jax.experimental.pallas import tpu as pltpu
from jax.sharding import PartitionSpec as P

BASIS = 64
RIM = 4
EXT = 16
EXT3 = 4096
XC_COEF = 0.9847450218426965
GRID_WEIGHT = 0.015625
G = 7
ROWS = G * BASIS
WIDE = 512
N = 8
OWNERS = N * N
PAIRS = 48
CODES = 56
ROW_BLK = 32
MESH = pl.DeviceIdType.MESH
F32 = jnp.float32
BF16 = jnp.bfloat16

CHUNK = 2048
NCHUNK = EXT3 // CHUNK

DIRS = [(a, b, c) for c in (0, 1, -1) for a in (0, 1, -1) for b in (0, 1, -1) if (a, b, c) != (0, 0, 0)]
DIR_ID = {d: n for n, d in enumerate(DIRS)}
OUT_PLANE = [d for d in DIRS if d[2] != 0]
FAR_Z = (2, 3, 4, 5, 6)
PEERS = OWNERS - 1 + len(OUT_PLANE) + len(FAR_Z)
FAR_FIRST = (4, 3, 5, 2, 6, 1, 7, 0)
SECOND = 3
FLAG = 128


def half(step, low, high, whole):
    return whole if step == 0 else (high if step > 0 else low)


def bytes_wait(ref, sem):
    pltpu.make_async_copy(ref, ref, sem).wait()


def main_kernel(
    basis_ref, blocks_ref, groups_ref, owner_ref, slot_ref,
    recv_ref, recv2_ref, slots_out, flag_out, pot_ref, table_ref,
    phi, wgt, blk, gv, ov, sv, a3, mperm, mat, rho, hr, vpot, kb, table, send, z2s, z2r, x2s,
    selv, sels, meta, mz, xs, mx, fl, fr, potv, slotv,
    load_sem, own_sem, halo_send, halo_recv, mz_send, mz_recv, mx_send, mx_recv, blk_send, blk_recv,
    z2_send, z2_recv, x2_send, x2_recv, fl_send, fl_recv,
):
    i = lax.axis_index("gx")
    j = lax.axis_index("gy")
    k = lax.axis_index("gz")
    me = i * N + j

    small = []
    for n, (src, dst) in enumerate(((groups_ref, gv), (owner_ref, ov), (slot_ref, sv), (blocks_ref, blk))):
        copy = pltpu.make_async_copy(src, dst, load_sem.at[NCHUNK + n])
        copy.start()
        small.append(copy)
    loads = []
    for n in range(NCHUNK):
        cols = pl.ds(n * CHUNK, CHUNK)
        copy = pltpu.make_async_copy(basis_ref.at[:, cols], phi.at[:, cols], load_sem.at[n])
        copy.start()
        loads.append(copy)

    barrier = pltpu.get_barrier_semaphore()

    def greet(t, carry):
        pl.semaphore_signal(
            barrier, inc=1,
            device_id=(lax.rem(i + t // N, N), lax.rem(j + lax.rem(t, N), N), k),
            device_id_type=MESH,
        )
        return carry

    lax.fori_loop(1, OWNERS, greet, 0)
    for a, b, c in OUT_PLANE + [(0, 0, t) for t in FAR_Z]:
        pl.semaphore_signal(
            barrier, inc=1,
            device_id=(lax.rem(i + a + N, N), lax.rem(j + b + N, N), lax.rem(k + c + N, N)),
            device_id_type=MESH,
        )

    lane = lax.broadcasted_iota(jnp.int32, (ROW_BLK, 128), 1)
    low = lane < BASIS
    r64 = lax.broadcasted_iota(jnp.int32, (BASIS, BASIS), 0)
    c64 = lax.broadcasted_iota(jnp.int32, (BASIS, BASIS), 1)
    split_rows = jnp.where(c64 == 2 * (r64 % 32) + r64 // 32, 1.0, 0.0).astype(BF16)
    join_rows = jnp.where(r64 == 2 * (c64 % 32) + c64 // 32, 1.0, 0.0).astype(BF16)

    small[0].wait()
    codes = gv[0:1, :] * G + gv[1:2, :]
    pick = jnp.where(
        lax.broadcasted_iota(jnp.int32, (CODES, PAIRS), 0) == codes, 1.0, 0.0
    ).astype(BF16)
    small[3].wait()
    for n in range(8):
        part = jnp.dot(pick, blk[:, n * 512:(n + 1) * 512], preferred_element_type=F32)
        for q in range(4):
            a3[pl.ds(n * 4 + q, CODES, stride=ROW_BLK), :] = part[:, q * 128:(q + 1) * 128]
    for a in range(G):
        for bp in range(4):
            even = a3[(a * G + 2 * bp) * ROW_BLK:(a * G + 2 * bp + 1) * ROW_BLK, :]
            if 2 * bp + 1 < G:
                odd = a3[(a * G + 2 * bp + 1) * ROW_BLK:(a * G + 2 * bp + 2) * ROW_BLK, :]
            else:
                odd = jnp.zeros((ROW_BLK, 128), F32)
            top = jnp.where(low, even, pltpu.roll(odd, 64, axis=1))
            bottom = jnp.where(low, pltpu.roll(even, 64, axis=1), odd)
            mperm[a * 64:a * 64 + 32, bp * 128:(bp + 1) * 128] = top.astype(BF16)
            mperm[a * 64 + 32:(a + 1) * 64, bp * 128:(bp + 1) * 128] = bottom.astype(BF16)
        mat[a * 64:(a + 1) * 64, :] = jnp.dot(
            join_rows, mperm[a * 64:(a + 1) * 64, :], preferred_element_type=F32
        ).astype(BF16)

    for n in range(NCHUNK):
        loads[n].wait()
        cols = slice(n * CHUNK, (n + 1) * CHUNK)
        part = phi[:, cols]
        image = jnp.dot(mat[:, :ROWS], part, preferred_element_type=F32)
        line = jnp.sum(part.astype(F32) * image, axis=0, keepdims=True)
        for q in range(CHUNK // 256):
            x = n * (CHUNK // 256) + q
            rho[x:x + 1, :] = line[:, q * 256:(q + 1) * 256]

    pl.semaphore_wait(barrier, PEERS)

    for n, (a, b, c) in enumerate(DIRS):
        src = rho.at[half(a, pl.ds(0, 8), pl.ds(8, 8), pl.ds(0, 16)),
                     half(b, pl.ds(0, 128), pl.ds(128, 128), pl.ds(0, 256))]
        dst = hr.at[n, half(-a, pl.ds(0, 8), pl.ds(8, 8), pl.ds(0, 16)),
                    half(-b, pl.ds(0, 128), pl.ds(128, 128), pl.ds(0, 256))]
        pltpu.make_async_remote_copy(
            src_ref=src, dst_ref=dst, send_sem=halo_send, recv_sem=halo_recv,
            device_id=(lax.rem(i + a + N, N), lax.rem(j + b + N, N), lax.rem(k + c + N, N)),
            device_id_type=MESH,
        ).start()

    for copy in small[1:3]:
        copy.wait()
    row = lax.broadcasted_iota(jnp.int32, (PAIRS, PAIRS), 0)
    col = lax.broadcasted_iota(jnp.int32, (PAIRS, PAIRS), 1)

    def upright(line):
        return jnp.sum(jnp.where(row == col, line, 0), axis=1, keepdims=True)

    def count(mask, axis):
        return jnp.sum(jnp.where(mask, 1, 0), axis=axis, keepdims=True)

    own_r = ov[...]
    own_c = upright(own_r)
    code_c = upright(codes)
    grp_r = own_r // N
    grp_c = own_c // N
    same = own_c == own_r
    rank_c = count(same & (col < row), 1)
    rank_r = count(same & (row < col), 0)
    mates = grp_c == grp_r
    idx_c = count(mates & (own_r < own_c) & (rank_r > 0), 1)
    idx_r = count(mates & (own_c < own_r) & (rank_c > 0), 0)
    place_c = rank_c * OWNERS + own_c
    place_r = rank_r * OWNERS + own_r
    wide = lax.broadcasted_iota(jnp.int32, (PAIRS, 128), 1)
    sel1 = jnp.sum(jnp.where(wide == place_c, code_c, 0), axis=0, keepdims=True)
    second_at = jnp.where((rank_c > 0) & (idx_c < SECOND), grp_c * SECOND + idx_c, -1)
    sel2 = jnp.sum(jnp.where(wide == second_at, code_c, 0), axis=0, keepdims=True)
    selv[0:1, :] = sel1
    selv[1:2, :] = sel2
    sel_copy = pltpu.make_async_copy(selv, sels, own_sem.at[0])
    sel_copy.start()
    tall = lax.broadcasted_iota(jnp.int32, (OWNERS, PAIRS), 0)
    first_m = tall == place_r
    second_m = tall + OWNERS == place_r
    first_slot = jnp.sum(jnp.where(first_m, sv[...] + 1, 0), axis=1, keepdims=True) - 1
    second_slot = jnp.sum(jnp.where(second_m, sv[...] + 1, 0), axis=1, keepdims=True) - 1
    second_idx = jnp.sum(jnp.where(second_m, idx_r + 1, 0), axis=1, keepdims=True) - 1
    over = jnp.max(jnp.where((rank_r > 0) & (idx_r >= SECOND), FLAG, 0), axis=1, keepdims=True)
    wide64 = lax.broadcasted_iota(jnp.int32, (OWNERS, 128), 1)
    tile = jnp.where(wide64 < OWNERS, first_slot + over, second_slot)
    index = jnp.broadcast_to(second_idx, (OWNERS, 128))
    for t in range(N):
        meta[t, 0] = tile[t * N:(t + 1) * N]
        meta[t, 1] = index[t * N:(t + 1) * N]

    def send_z(t, carry):
        ti = lax.rem(i + t, N)
        pltpu.make_async_remote_copy(
            src_ref=meta.at[ti], dst_ref=mz.at[i], send_sem=mz_send, recv_sem=mz_recv,
            device_id=(ti, j, k), device_id_type=MESH,
        ).start()
        return carry

    lax.fori_loop(1, N, send_z, 0)
    mz[i] = meta[i]

    bytes_wait(hr.at[0:11], halo_recv)
    zlow = lax.rem(lax.broadcasted_iota(jnp.int32, (8, 128), 1), EXT) < 8
    for hx in range(2):
        for hy in range(2):
            rows = slice(hx * 8, hx * 8 + 8)
            cols = slice(hy * 128, hy * 128 + 128)
            total = rho[rows, cols]
            steps_x = (0, 1 - 2 * hx)
            steps_y = (0, 1 - 2 * hy)
            for a in steps_x:
                for b in steps_y:
                    if (a, b) != (0, 0):
                        total = total + hr[DIR_ID[(a, b, 0)], rows, cols]
            sides = []
            for c in (1, -1):
                side = None
                for a in steps_x:
                    for b in steps_y:
                        term = hr[DIR_ID[(a, b, c)], rows, cols]
                        side = term if side is None else side + term
                sides.append(side)
            total = total + jnp.where(
                zlow, pltpu.roll(sides[0], 120, axis=1), pltpu.roll(sides[1], 8, axis=1)
            )
            cubic = jnp.exp(jnp.log(total * total + 1.0) * (-1.0 / 3.0))
            vpot[rows, cols] = -XC_COEF * total * cubic
    left = vpot[4:12, 0:128]
    right = vpot[4:12, 128:256]
    lane8 = lax.broadcasted_iota(jnp.int32, (8, 128), 1)
    potv[...] = jnp.where(
        lane8 < 64, pltpu.roll(left, 64, axis=1), pltpu.roll(right, 64, axis=1)
    )
    pot_copy = pltpu.make_async_copy(potv, pot_ref, own_sem.at[3])
    pot_copy.start()

    for x in range(EXT):
        cols = slice(x * 256, (x + 1) * 256)
        wgt[:, cols] = (phi[:, cols].astype(F32) * vpot[x:x + 1, :]).astype(BF16)
    ks = lax.dot_general(
        wgt[...], phi[...], (((1,), (1,)), ((), ())), preferred_element_type=F32
    )
    kb[:, 0:ROWS] = (ks * GRID_WEIGHT).astype(BF16)
    kb[:, ROWS:] = jnp.zeros((ROWS, WIDE - ROWS), BF16)
    for a in range(G):
        rows = jnp.dot(split_rows, kb[a * 64:(a + 1) * 64, :], preferred_element_type=F32)
        for bp in range(4):
            top = rows[0:32, bp * 128:(bp + 1) * 128]
            bottom = rows[32:64, bp * 128:(bp + 1) * 128]
            table[a * G + 2 * bp] = jnp.where(low, top, pltpu.roll(bottom, 64, axis=1)).astype(BF16)
            if 2 * bp + 1 < G:
                table[a * G + 2 * bp + 1] = jnp.where(
                    low, pltpu.roll(top, 64, axis=1), bottom
                ).astype(BF16)

    bytes_wait(mz.at[0:N - 1], mz_recv)
    for t in range(N):
        xs[t] = mz[:, 0, t, :]

    def send_x(t, carry):
        tj = lax.rem(j + t, N)
        pltpu.make_async_remote_copy(
            src_ref=xs.at[tj], dst_ref=mx.at[j], send_sem=mx_send, recv_sem=mx_recv,
            device_id=(i, tj, k), device_id_type=MESH,
        ).start()
        return carry

    lax.fori_loop(1, N, send_x, 0)
    mx[j] = xs[j]

    sel_copy.wait()
    keep = pltpu.make_async_copy(table, table_ref, own_sem.at[0])
    keep.start()

    def pack_second(t, carry):
        for c in range(SECOND):
            z2s[t, c] = table[sels[1, t * SECOND + c]]
        return carry

    lax.fori_loop(0, N, pack_second, 0)

    def send_second(t, carry):
        ti = lax.rem(i + t, N)
        pltpu.make_async_remote_copy(
            src_ref=z2s.at[ti], dst_ref=z2r.at[i], send_sem=z2_send, recv_sem=z2_recv,
            device_id=(ti, j, k), device_id_type=MESH,
        ).start()
        return carry

    lax.fori_loop(1, N, send_second, 0)
    z2r[i] = z2s[i]

    for di in FAR_FIRST:
        ti = lax.rem(i + di, N)

        def send_block(t, carry, ti=ti):
            tj = lax.rem(j + t, N)
            target = ti * N + tj
            send[target] = table[sels[0, target]]
            pltpu.make_async_remote_copy(
                src_ref=send.at[target], dst_ref=recv_ref.at[me], send_sem=blk_send,
                recv_sem=blk_recv, device_id=(ti, tj, k), device_id_type=MESH,
            ).start()
            return carry

        lax.fori_loop(0 if di else 1, N, send_block, 0)
    send[me] = table[sels[0, me]]
    own = pltpu.make_async_copy(send.at[me], recv_ref.at[me], own_sem.at[1])
    own.start()

    bytes_wait(mx.at[0:N - 1], mx_recv)
    wide8 = lax.broadcasted_iota(jnp.int32, (N, 128), 1)
    sub8 = lax.broadcasted_iota(jnp.int32, (N, 128), 0)
    slots = jnp.zeros((N, 128), jnp.int32)
    over = jnp.zeros((N, 128), jnp.int32)
    for t in range(N):
        part = mx[t]
        left_over = (wide8 < OWNERS) & (part >= FLAG - 1)
        over = jnp.maximum(over, jnp.where(left_over, 1, 0))
        value = jnp.where(left_over, part - FLAG, part)
        here = (wide8 == sub8 * N + t) | (wide8 == OWNERS + t * N + sub8)
        slots = slots + jnp.where(here, value, 0)
    slotv[...] = jnp.broadcast_to(jnp.sum(slots, axis=0, keepdims=True), (N, 128))
    slot_copy = pltpu.make_async_copy(slotv, slots_out, own_sem.at[4])
    slot_copy.start()
    fl[...] = over

    def send_flag(t, carry):
        tk = lax.rem(k + t, N)
        pltpu.make_async_remote_copy(
            src_ref=fl, dst_ref=fr.at[k], send_sem=fl_send, recv_sem=fl_recv,
            device_id=(i, j, tk), device_id_type=MESH,
        ).start()
        return carry

    lax.fori_loop(1, N, send_flag, 0)
    fr[k] = over

    bytes_wait(z2r.at[0:N - 1], z2_recv)
    for t in range(N):
        def place_second(a, carry, t=t):
            index = jnp.broadcast_to(mz[a, 1, t:t + 1, :], (ROW_BLK, 128))
            total = jnp.zeros((ROW_BLK, 128), F32)
            for c in range(SECOND):
                total = jnp.where(index == c, z2r[a, c].astype(F32), total)
            x2s[t, a] = total.astype(BF16)
            return carry

        lax.fori_loop(0, N, place_second, 0)

    def forward(t, carry):
        tj = lax.rem(j + t, N)
        pltpu.make_async_remote_copy(
            src_ref=x2s.at[tj], dst_ref=recv2_ref.at[j], send_sem=x2_send, recv_sem=x2_recv,
            device_id=(i, tj, k), device_id_type=MESH,
        ).start()
        return carry

    lax.fori_loop(1, N, forward, 0)
    own2 = pltpu.make_async_copy(x2s.at[j], recv2_ref.at[j], own_sem.at[2])
    own2.start()

    bytes_wait(fr.at[0:N - 1], fl_recv)
    for t in range(N):
        over = jnp.maximum(over, fr[t])
    flag_out[...] = jnp.max(jnp.max(over, axis=0, keepdims=True), axis=1, keepdims=True)

    for copy in (keep, pot_copy, slot_copy):
        copy.wait()
    own.wait()
    own2.wait()
    bytes_wait(fr.at[0:N - 1], fl_send)
    bytes_wait(xs.at[0:N - 1], mx_send)
    bytes_wait(mz.at[0:N - 1], mz_send)
    bytes_wait(hr.at[0:11], halo_send)
    bytes_wait(z2s.at[0:N - 1], z2_send)
    bytes_wait(x2s.at[0:N - 1], x2_send)
    bytes_wait(send.at[0:OWNERS - 1], blk_send)
    bytes_wait(recv2_ref.at[0:N - 1], x2_recv)
    bytes_wait(recv_ref.at[0:OWNERS - 1], blk_recv)


def store_kernel(slots_ref, recv_ref, recv2_ref, pot_ref, out_ref, pot_out, acc):
    acc[...] = jnp.zeros_like(acc)
    pot = pot_ref[...]
    for y in range(8):
        pot_out[:, y, :] = pot[:, y * EXT + RIM:y * EXT + RIM + 8]

    def add(t, carry):
        for rank, ref in enumerate((recv_ref, recv2_ref)):
            slot = slots_ref[0, rank * OWNERS + t]
            slot = jnp.where(slot < 0, PAIRS, slot)
            at = pl.ds(pl.multiple_of(slot * ROW_BLK, ROW_BLK), ROW_BLK)
            acc[at, :] += ref[t].astype(F32)
        return carry

    lax.fori_loop(0, OWNERS, add, 0, unroll=4)
    for c in range(ROW_BLK):
        out_ref[:, c * 128:(c + 1) * 128] = acc[pl.ds(c, PAIRS, stride=ROW_BLK), :].astype(BF16)


def store(slots, recv, recv2, pot):
    vmem = pl.BlockSpec(memory_space=pltpu.VMEM)
    smem = pl.BlockSpec(memory_space=pltpu.SMEM)
    return pl.pallas_call(
        store_kernel,
        name="store_blocks",
        out_shape=(
            jax.ShapeDtypeStruct((PAIRS, 4096), BF16),
            jax.ShapeDtypeStruct((8, 8, 8), F32),
        ),
        in_specs=[smem, vmem, vmem, vmem],
        out_specs=(vmem, vmem),
        scratch_shapes=[pltpu.VMEM(((PAIRS + 1) * ROW_BLK, 128), F32)],
        compiler_params=pltpu.CompilerParams(vmem_limit_bytes=16 << 20),
    )(slots, recv, recv2, pot)


def resend(pair_groups, owner, owner_slot, table, slots, recv, recv2, pot):
    codes = pair_groups[0] * G + pair_groups[1]
    names = owner[:, 0]
    order = jnp.arange(PAIRS, dtype=jnp.int32)
    earlier = (names[:, None] == names[None, :]) & (order[:, None] > order[None, :])
    rank = jnp.sum(earlier.astype(jnp.int32), axis=1)
    match = (jnp.arange(OWNERS, dtype=jnp.int32)[:, None] == names[None, :]) & (rank[None, :] == 1)
    pick = jnp.sum(jnp.where(match, codes[None, :], 0), axis=1)
    second = jnp.sum(jnp.where(match, owner_slot[None, :] + 1, 0), axis=1) - 1
    chosen = (jnp.arange(G * G, dtype=jnp.int32)[None, :] == pick[:, None]).astype(BF16)
    blocks = lax.dot_general(
        chosen, table, (((1,), (0,)), ((), ())), preferred_element_type=F32
    ).astype(BF16)
    got = lax.all_to_all(blocks, ("gx", "gy"), split_axis=0, concat_axis=0, tiled=True)
    got_slots = lax.all_to_all(second, ("gx", "gy"), split_axis=0, concat_axis=0, tiled=True)
    new = jnp.concatenate([slots[:, :OWNERS], jnp.broadcast_to(got_slots[None], (N, OWNERS))], axis=1)
    return store(new, recv, got, pot)


def per_device(basis, density_blocks, pair_groups, owner, owner_slot):
    vmem = pl.BlockSpec(memory_space=pltpu.VMEM)
    hbm = pl.BlockSpec(memory_space=pl.ANY)
    block = (ROW_BLK, 128)
    dma = pltpu.SemaphoreType.DMA
    recv, recv2, slots, flag, pot, table = pl.pallas_call(
        main_kernel,
        name="collocate_exchange",
        out_shape=(
            jax.ShapeDtypeStruct((OWNERS, *block), BF16),
            jax.ShapeDtypeStruct((N, N, *block), BF16),
            jax.ShapeDtypeStruct((N, 128), jnp.int32),
            jax.ShapeDtypeStruct((1, 1), jnp.int32),
            jax.ShapeDtypeStruct((8, 128), F32),
            jax.ShapeDtypeStruct((G * G, *block), BF16),
        ),
        in_specs=[hbm] * 5,
        out_specs=(hbm, hbm, hbm, vmem, hbm, hbm),
        scratch_shapes=[
            pltpu.VMEM((ROWS, EXT3), BF16),
            pltpu.VMEM((ROWS, EXT3), BF16),
            pltpu.VMEM((PAIRS, 4096), BF16),
            pltpu.VMEM((2, PAIRS), jnp.int32),
            pltpu.VMEM((1, PAIRS), jnp.int32),
            pltpu.VMEM((1, PAIRS), jnp.int32),
            pltpu.VMEM((CODES * ROW_BLK, 128), F32),
            pltpu.VMEM((ROWS, WIDE), BF16),
            pltpu.VMEM((ROWS, WIDE), BF16),
            pltpu.VMEM((EXT, 256), F32),
            pltpu.VMEM((len(DIRS), EXT, 256), F32),
            pltpu.VMEM((EXT, 256), F32),
            pltpu.VMEM((ROWS, WIDE), BF16),
            pltpu.VMEM((G * G, *block), BF16),
            pltpu.VMEM((OWNERS, *block), BF16),
            pltpu.VMEM((N, SECOND, *block), BF16),
            pltpu.VMEM((N, SECOND, *block), BF16),
            pltpu.VMEM((N, N, *block), BF16),
            pltpu.VMEM((2, 128), jnp.int32),
            pltpu.SMEM((2, 128), jnp.int32),
            pltpu.VMEM((N, 2, N, 128), jnp.int32),
            pltpu.VMEM((N, 2, N, 128), jnp.int32),
            pltpu.VMEM((N, N, 128), jnp.int32),
            pltpu.VMEM((N, N, 128), jnp.int32),
            pltpu.VMEM((N, 128), jnp.int32),
            pltpu.VMEM((N, N, 128), jnp.int32),
            pltpu.VMEM((8, 128), F32),
            pltpu.VMEM((N, 128), jnp.int32),
            dma((NCHUNK + 4,)),
            dma((5,)),
        ] + [dma] * 14,
        compiler_params=pltpu.CompilerParams(
            collective_id=1, has_side_effects=True, vmem_limit_bytes=61 << 20
        ),
        cost_estimate=pl.CostEstimate(
            flops=4 * ROWS * ROWS * EXT3, bytes_accessed=6 << 20, transcendentals=2 * EXT3
        ),
    )(
        basis.reshape(ROWS, EXT3), density_blocks, pair_groups,
        owner.reshape(1, PAIRS), owner_slot.reshape(1, PAIRS),
    )
    recv2 = recv2.reshape(OWNERS, *block)
    return lax.cond(
        flag[0, 0] > 0,
        lambda: resend(pair_groups, owner, owner_slot, table, slots, recv, recv2, pot),
        lambda: store(slots, recv, recv2, pot),
    )


def solution(mesh):
    return jax.shard_map(
        per_device,
        mesh=mesh,
        in_specs=(
            P(("gx", "gy", "gz"), None, None),
            P(("gx", "gy", "gz"), None),
            P(None, ("gx", "gy", "gz")),
            P(("gx", "gy", "gz"), None),
            P(("gx", "gy", "gz")),
        ),
        out_specs=(P(("gx", "gy", "gz"), None), P("gx", "gy", "gz")),
        check_vma=False,
    )
```

```python
import functools

import jax
import jax.numpy as jnp
from jax import lax
from jax.experimental import pallas as pl
from jax.experimental.pallas import tpu as pltpu
from jax.sharding import PartitionSpec as P

BASIS = 64
RIM = 4
EXT = 16
EXT3 = 4096
XC_COEF = 0.9847450218426965
GRID_WEIGHT = 0.015625
G = 7
ROWS = G * BASIS
WIDE = 512
N = 8
OWNERS = N * N
PAIRS = 48
CODES = 56
ROW_BLK = 32
MESH = pl.DeviceIdType.MESH
F32 = jnp.float32
BF16 = jnp.bfloat16

CHUNK = 2048
NCHUNK = EXT3 // CHUNK

DIRS = [(a, b, c) for c in (0, 1, -1) for a in (0, 1, -1) for b in (0, 1, -1) if (a, b, c) != (0, 0, 0)]
DIR_ID = {d: n for n, d in enumerate(DIRS)}
OUT_PLANE = [d for d in DIRS if d[2] != 0]
FAR_Z = (2, 3, 4, 5, 6)
PEERS = OWNERS - 1 + len(OUT_PLANE) + len(FAR_Z)
FAR_FIRST = (4, 3, 5, 2, 6, 1, 7, 0)
SECOND = 3
FLAG = 128


def half(step, low, high, whole):
    return whole if step == 0 else (high if step > 0 else low)


def bytes_wait(ref, sem):
    pltpu.make_async_copy(ref, ref, sem).wait()


def main_kernel(
    basis_ref, blocks_ref, groups_ref, owner_ref, slot_ref,
    recv_ref, recv2_ref, slots_out, flag_out, pot_ref, table_ref,
    phi, wgt, blk, gv, ov, sv, a3, mperm, mat, rho, hr, vpot, kb, table, send, z2s, z2r, x2s,
    selv, sels, meta, mz, xs, mx, fl, fr, potv, slotv,
    load_sem, own_sem, halo_send, halo_recv, mz_send, mz_recv, mx_send, mx_recv, blk_send, blk_recv,
    z2_send, z2_recv, x2_send, x2_recv, fl_send, fl_recv,
):
    i = lax.axis_index("gx")
    j = lax.axis_index("gy")
    k = lax.axis_index("gz")
    me = i * N + j

    small = []
    for n, (src, dst) in enumerate(((groups_ref, gv), (owner_ref, ov), (slot_ref, sv), (blocks_ref, blk))):
        copy = pltpu.make_async_copy(src, dst, load_sem.at[NCHUNK + n])
        copy.start()
        small.append(copy)
    loads = []
    for n in range(NCHUNK):
        cols = pl.ds(n * CHUNK, CHUNK)
        copy = pltpu.make_async_copy(basis_ref.at[:, cols], phi.at[:, cols], load_sem.at[n])
        copy.start()
        loads.append(copy)

    barrier = pltpu.get_barrier_semaphore()
    gxs = [lax.rem(i + t, N) for t in range(N)]
    gys = [lax.rem(j + t, N) for t in range(N)]
    gzs = [lax.rem(k + t, N) for t in range(N)]
    peers = [(a % N, b % N, c % N) for a, b, c in OUT_PLANE + [(0, 0, t) for t in FAR_Z]]
    peers += [(a, b, 0) for a in FAR_FIRST for b in (4, 3, 5, 2, 6, 1, 7, 0) if (a, b) != (0, 0)]
    for a, b, c in peers:
        pl.semaphore_signal(
            barrier, inc=1, device_id=(gxs[a], gys[b], gzs[c]), device_id_type=MESH
        )

    lane = lax.broadcasted_iota(jnp.int32, (ROW_BLK, 128), 1)
    low = lane < BASIS
    r64 = lax.broadcasted_iota(jnp.int32, (BASIS, BASIS), 0)
    c64 = lax.broadcasted_iota(jnp.int32, (BASIS, BASIS), 1)
    split_rows = jnp.where(c64 == 2 * (r64 % 32) + r64 // 32, 1.0, 0.0).astype(BF16)
    join_rows = jnp.where(r64 == 2 * (c64 % 32) + c64 // 32, 1.0, 0.0).astype(BF16)

    small[0].wait()
    codes = gv[0:1, :] * G + gv[1:2, :]
    pick = jnp.where(
        lax.broadcasted_iota(jnp.int32, (CODES, PAIRS), 0) == codes, 1.0, 0.0
    ).astype(BF16)
    small[3].wait()
    for n in range(8):
        part = jnp.dot(pick, blk[:, n * 512:(n + 1) * 512], preferred_element_type=F32)
        for q in range(4):
            a3[pl.ds(n * 4 + q, CODES, stride=ROW_BLK), :] = part[:, q * 128:(q + 1) * 128]
    for a in range(G):
        for bp in range(4):
            even = a3[(a * G + 2 * bp) * ROW_BLK:(a * G + 2 * bp + 1) * ROW_BLK, :]
            if 2 * bp + 1 < G:
                odd = a3[(a * G + 2 * bp + 1) * ROW_BLK:(a * G + 2 * bp + 2) * ROW_BLK, :]
            else:
                odd = jnp.zeros((ROW_BLK, 128), F32)
            top = jnp.where(low, even, pltpu.roll(odd, 64, axis=1))
            bottom = jnp.where(low, pltpu.roll(even, 64, axis=1), odd)
            mperm[a * 64:a * 64 + 32, bp * 128:(bp + 1) * 128] = top.astype(BF16)
            mperm[a * 64 + 32:(a + 1) * 64, bp * 128:(bp + 1) * 128] = bottom.astype(BF16)
        mat[a * 64:(a + 1) * 64, :] = jnp.dot(
            join_rows, mperm[a * 64:(a + 1) * 64, :], preferred_element_type=F32
        ).astype(BF16)

    for n in range(NCHUNK):
        loads[n].wait()
        cols = slice(n * CHUNK, (n + 1) * CHUNK)
        part = phi[:, cols]
        image = jnp.dot(mat[:, :ROWS], part, preferred_element_type=F32)
        line = jnp.sum(part.astype(F32) * image, axis=0, keepdims=True)
        for q in range(CHUNK // 256):
            x = n * (CHUNK // 256) + q
            rho[x:x + 1, :] = line[:, q * 256:(q + 1) * 256]

    pl.semaphore_wait(barrier, PEERS)

    for n, (a, b, c) in enumerate(DIRS):
        src = rho.at[half(a, pl.ds(0, 8), pl.ds(8, 8), pl.ds(0, 16)),
                     half(b, pl.ds(0, 128), pl.ds(128, 128), pl.ds(0, 256))]
        dst = hr.at[n, half(-a, pl.ds(0, 8), pl.ds(8, 8), pl.ds(0, 16)),
                    half(-b, pl.ds(0, 128), pl.ds(128, 128), pl.ds(0, 256))]
        pltpu.make_async_remote_copy(
            src_ref=src, dst_ref=dst, send_sem=halo_send, recv_sem=halo_recv,
            device_id=(lax.rem(i + a + N, N), lax.rem(j + b + N, N), lax.rem(k + c + N, N)),
            device_id_type=MESH,
        ).start()

    for copy in small[1:3]:
        copy.wait()
    row = lax.broadcasted_iota(jnp.int32, (PAIRS, PAIRS), 0)
    col = lax.broadcasted_iota(jnp.int32, (PAIRS, PAIRS), 1)

    def upright(line):
        return jnp.sum(jnp.where(row == col, line, 0), axis=1, keepdims=True)

    def count(mask, axis):
        return jnp.sum(jnp.where(mask, 1, 0), axis=axis, keepdims=True)

    own_r = ov[...]
    own_c = upright(own_r)
    code_c = upright(codes)
    grp_r = own_r // N
    grp_c = own_c // N
    same = own_c == own_r
    rank_c = count(same & (col < row), 1)
    rank_r = count(same & (row < col), 0)
    mates = grp_c == grp_r
    idx_c = count(mates & (own_r < own_c) & (rank_r > 0), 1)
    idx_r = count(mates & (own_c < own_r) & (rank_c > 0), 0)
    place_c = rank_c * OWNERS + own_c
    place_r = rank_r * OWNERS + own_r
    wide = lax.broadcasted_iota(jnp.int32, (PAIRS, 128), 1)
    sel1 = jnp.sum(jnp.where(wide == place_c, code_c, 0), axis=0, keepdims=True)
    second_at = jnp.where((rank_c > 0) & (idx_c < SECOND), grp_c * SECOND + idx_c, -1)
    sel2 = jnp.sum(jnp.where(wide == second_at, code_c, 0), axis=0, keepdims=True)
    selv[0:1, :] = sel1
    selv[1:2, :] = sel2
    sel_copy = pltpu.make_async_copy(selv, sels, own_sem.at[0])
    sel_copy.start()
    tall = lax.broadcasted_iota(jnp.int32, (OWNERS, PAIRS), 0)
    first_m = tall == place_r
    second_m = tall + OWNERS == place_r
    first_slot = jnp.sum(jnp.where(first_m, sv[...] + 1, 0), axis=1, keepdims=True) - 1
    second_slot = jnp.sum(jnp.where(second_m, sv[...] + 1, 0), axis=1, keepdims=True) - 1
    second_idx = jnp.sum(jnp.where(second_m, idx_r + 1, 0), axis=1, keepdims=True) - 1
    over = jnp.max(jnp.where((rank_r > 0) & (idx_r >= SECOND), FLAG, 0), axis=1, keepdims=True)
    wide64 = lax.broadcasted_iota(jnp.int32, (OWNERS, 128), 1)
    tile = jnp.where(wide64 < OWNERS, first_slot + over, second_slot)
    index = jnp.broadcast_to(second_idx, (OWNERS, 128))
    for t in range(N):
        meta[t, 0] = tile[t * N:(t + 1) * N]
        meta[t, 1] = index[t * N:(t + 1) * N]

    def send_z(t, carry):
        ti = lax.rem(i + t, N)
        pltpu.make_async_remote_copy(
            src_ref=meta.at[ti], dst_ref=mz.at[i], send_sem=mz_send, recv_sem=mz_recv,
            device_id=(ti, j, k), device_id_type=MESH,
        ).start()
        return carry

    lax.fori_loop(1, N, send_z, 0)
    mz[i] = meta[i]

    bytes_wait(hr.at[0:11], halo_recv)
    zlow = lax.rem(lax.broadcasted_iota(jnp.int32, (8, 128), 1), EXT) < 8
    for hx in range(2):
        for hy in range(2):
            rows = slice(hx * 8, hx * 8 + 8)
            cols = slice(hy * 128, hy * 128 + 128)
            total = rho[rows, cols]
            steps_x = (0, 1 - 2 * hx)
            steps_y = (0, 1 - 2 * hy)
            for a in steps_x:
                for b in steps_y:
                    if (a, b) != (0, 0):
                        total = total + hr[DIR_ID[(a, b, 0)], rows, cols]
            sides = []
            for c in (1, -1):
                side = None
                for a in steps_x:
                    for b in steps_y:
                        term = hr[DIR_ID[(a, b, c)], rows, cols]
                        side = term if side is None else side + term
                sides.append(side)
            total = total + jnp.where(
                zlow, pltpu.roll(sides[0], 120, axis=1), pltpu.roll(sides[1], 8, axis=1)
            )
            cubic = jnp.exp(jnp.log(total * total + 1.0) * (-1.0 / 3.0))
            vpot[rows, cols] = -XC_COEF * total * cubic
    left = vpot[4:12, 0:128]
    right = vpot[4:12, 128:256]
    lane8 = lax.broadcasted_iota(jnp.int32, (8, 128), 1)
    potv[...] = jnp.where(
        lane8 < 64, pltpu.roll(left, 64, axis=1), pltpu.roll(right, 64, axis=1)
    )
    pot_copy = pltpu.make_async_copy(potv, pot_ref, own_sem.at[3])
    pot_copy.start()

    for x in range(EXT):
        cols = slice(x * 256, (x + 1) * 256)
        wgt[:, cols] = (phi[:, cols].astype(F32) * vpot[x:x + 1, :]).astype(BF16)
    ks = lax.dot_general(
        wgt[...], phi[...], (((1,), (1,)), ((), ())), preferred_element_type=F32
    )
    kb[:, 0:ROWS] = (ks * GRID_WEIGHT).astype(BF16)
    kb[:, ROWS:] = jnp.zeros((ROWS, WIDE - ROWS), BF16)
    for a in range(G):
        rows = jnp.dot(split_rows, kb[a * 64:(a + 1) * 64, :], preferred_element_type=F32)
        for bp in range(4):
            top = rows[0:32, bp * 128:(bp + 1) * 128]
            bottom = rows[32:64, bp * 128:(bp + 1) * 128]
            table[a * G + 2 * bp] = jnp.where(low, top, pltpu.roll(bottom, 64, axis=1)).astype(BF16)
            if 2 * bp + 1 < G:
                table[a * G + 2 * bp + 1] = jnp.where(
                    low, pltpu.roll(top, 64, axis=1), bottom
                ).astype(BF16)

    bytes_wait(mz.at[0:N - 1], mz_recv)
    for t in range(N):
        xs[t] = mz[:, 0, t, :]

    def send_x(t, carry):
        tj = lax.rem(j + t, N)
        pltpu.make_async_remote_copy(
            src_ref=xs.at[tj], dst_ref=mx.at[j], send_sem=mx_send, recv_sem=mx_recv,
            device_id=(i, tj, k), device_id_type=MESH,
        ).start()
        return carry

    lax.fori_loop(1, N, send_x, 0)
    mx[j] = xs[j]

    sel_copy.wait()
    keep = pltpu.make_async_copy(table, table_ref, own_sem.at[0])
    keep.start()

    def pack_second(t, carry):
        for c in range(SECOND):
            z2s[t, c] = table[sels[1, t * SECOND + c]]
        return carry

    lax.fori_loop(0, N, pack_second, 0)

    def send_second(t, carry):
        ti = lax.rem(i + t, N)
        pltpu.make_async_remote_copy(
            src_ref=z2s.at[ti], dst_ref=z2r.at[i], send_sem=z2_send, recv_sem=z2_recv,
            device_id=(ti, j, k), device_id_type=MESH,
        ).start()
        return carry

    lax.fori_loop(1, N, send_second, 0)
    z2r[i] = z2s[i]

    for di in FAR_FIRST:
        ti = lax.rem(i + di, N)

        def send_block(t, carry, ti=ti):
            tj = lax.rem(j + t, N)
            target = ti * N + tj
            send[target] = table[sels[0, target]]
            pltpu.make_async_remote_copy(
                src_ref=send.at[target], dst_ref=recv_ref.at[me], send_sem=blk_send,
                recv_sem=blk_recv, device_id=(ti, tj, k), device_id_type=MESH,
            ).start()
            return carry

        lax.fori_loop(0 if di else 1, N, send_block, 0)
    send[me] = table[sels[0, me]]
    own = pltpu.make_async_copy(send.at[me], recv_ref.at[me], own_sem.at[1])
    own.start()

    bytes_wait(mx.at[0:N - 1], mx_recv)
    wide8 = lax.broadcasted_iota(jnp.int32, (N, 128), 1)
    sub8 = lax.broadcasted_iota(jnp.int32, (N, 128), 0)
    slots = jnp.zeros((N, 128), jnp.int32)
    over = jnp.zeros((N, 128), jnp.int32)
    for t in range(N):
        part = mx[t]
        left_over = (wide8 < OWNERS) & (part >= FLAG - 1)
        over = jnp.maximum(over, jnp.where(left_over, 1, 0))
        value = jnp.where(left_over, part - FLAG, part)
        here = (wide8 == sub8 * N + t) | (wide8 == OWNERS + t * N + sub8)
        slots = slots + jnp.where(here, value, 0)
    slotv[...] = jnp.broadcast_to(jnp.sum(slots, axis=0, keepdims=True), (N, 128))
    slot_copy = pltpu.make_async_copy(slotv, slots_out, own_sem.at[4])
    slot_copy.start()
    fl[...] = over

    def send_flag(t, carry):
        tk = lax.rem(k + t, N)
        pltpu.make_async_remote_copy(
            src_ref=fl, dst_ref=fr.at[k], send_sem=fl_send, recv_sem=fl_recv,
            device_id=(i, j, tk), device_id_type=MESH,
        ).start()
        return carry

    lax.fori_loop(1, N, send_flag, 0)
    fr[k] = over

    bytes_wait(z2r.at[0:N - 1], z2_recv)
    for t in range(N):
        def place_second(a, carry, t=t):
            index = jnp.broadcast_to(mz[a, 1, t:t + 1, :], (ROW_BLK, 128))
            total = jnp.zeros((ROW_BLK, 128), F32)
            for c in range(SECOND):
                total = jnp.where(index == c, z2r[a, c].astype(F32), total)
            x2s[t, a] = total.astype(BF16)
            return carry

        lax.fori_loop(0, N, place_second, 0)

    def forward(t, carry):
        tj = lax.rem(j + t, N)
        pltpu.make_async_remote_copy(
            src_ref=x2s.at[tj], dst_ref=recv2_ref.at[j], send_sem=x2_send, recv_sem=x2_recv,
            device_id=(i, tj, k), device_id_type=MESH,
        ).start()
        return carry

    lax.fori_loop(1, N, forward, 0)
    own2 = pltpu.make_async_copy(x2s.at[j], recv2_ref.at[j], own_sem.at[2])
    own2.start()

    bytes_wait(fr.at[0:N - 1], fl_recv)
    for t in range(N):
        over = jnp.maximum(over, fr[t])
    flag_out[...] = jnp.max(jnp.max(over, axis=0, keepdims=True), axis=1, keepdims=True)

    for copy in (keep, pot_copy, slot_copy):
        copy.wait()
    own.wait()
    own2.wait()
    bytes_wait(fr.at[0:N - 1], fl_send)
    bytes_wait(xs.at[0:N - 1], mx_send)
    bytes_wait(mz.at[0:N - 1], mz_send)
    bytes_wait(hr.at[0:11], halo_send)
    bytes_wait(z2s.at[0:N - 1], z2_send)
    bytes_wait(x2s.at[0:N - 1], x2_send)
    bytes_wait(send.at[0:OWNERS - 1], blk_send)
    bytes_wait(recv2_ref.at[0:N - 1], x2_recv)
    bytes_wait(recv_ref.at[0:OWNERS - 1], blk_recv)


def store_kernel(slots_ref, recv_ref, recv2_ref, pot_ref, out_ref, pot_out, acc):
    acc[...] = jnp.zeros_like(acc)
    pot = pot_ref[...]
    for y in range(8):
        pot_out[:, y, :] = pot[:, y * EXT + RIM:y * EXT + RIM + 8]

    def add(t, carry):
        for rank, ref in enumerate((recv_ref, recv2_ref)):
            slot = slots_ref[0, rank * OWNERS + t]
            slot = jnp.where(slot < 0, PAIRS, slot)
            at = pl.ds(pl.multiple_of(slot * ROW_BLK, ROW_BLK), ROW_BLK)
            acc[at, :] += ref[t].astype(F32)
        return carry

    lax.fori_loop(0, OWNERS, add, 0, unroll=4)
    for c in range(ROW_BLK):
        out_ref[:, c * 128:(c + 1) * 128] = acc[pl.ds(c, PAIRS, stride=ROW_BLK), :].astype(BF16)


def store(slots, recv, recv2, pot):
    vmem = pl.BlockSpec(memory_space=pltpu.VMEM)
    smem = pl.BlockSpec(memory_space=pltpu.SMEM)
    return pl.pallas_call(
        store_kernel,
        name="store_blocks",
        out_shape=(
            jax.ShapeDtypeStruct((PAIRS, 4096), BF16),
            jax.ShapeDtypeStruct((8, 8, 8), F32),
        ),
        in_specs=[smem, vmem, vmem, vmem],
        out_specs=(vmem, vmem),
        scratch_shapes=[pltpu.VMEM(((PAIRS + 1) * ROW_BLK, 128), F32)],
        compiler_params=pltpu.CompilerParams(vmem_limit_bytes=16 << 20),
    )(slots, recv, recv2, pot)


def resend(pair_groups, owner, owner_slot, table, slots, recv, recv2, pot):
    codes = pair_groups[0] * G + pair_groups[1]
    names = owner[:, 0]
    order = jnp.arange(PAIRS, dtype=jnp.int32)
    earlier = (names[:, None] == names[None, :]) & (order[:, None] > order[None, :])
    rank = jnp.sum(earlier.astype(jnp.int32), axis=1)
    match = (jnp.arange(OWNERS, dtype=jnp.int32)[:, None] == names[None, :]) & (rank[None, :] == 1)
    pick = jnp.sum(jnp.where(match, codes[None, :], 0), axis=1)
    second = jnp.sum(jnp.where(match, owner_slot[None, :] + 1, 0), axis=1) - 1
    chosen = (jnp.arange(G * G, dtype=jnp.int32)[None, :] == pick[:, None]).astype(BF16)
    blocks = lax.dot_general(
        chosen, table, (((1,), (0,)), ((), ())), preferred_element_type=F32
    ).astype(BF16)
    got = lax.all_to_all(blocks, ("gx", "gy"), split_axis=0, concat_axis=0, tiled=True)
    got_slots = lax.all_to_all(second, ("gx", "gy"), split_axis=0, concat_axis=0, tiled=True)
    new = jnp.concatenate([slots[:, :OWNERS], jnp.broadcast_to(got_slots[None], (N, OWNERS))], axis=1)
    return store(new, recv, got, pot)


def per_device(basis, density_blocks, pair_groups, owner, owner_slot):
    vmem = pl.BlockSpec(memory_space=pltpu.VMEM)
    hbm = pl.BlockSpec(memory_space=pl.ANY)
    block = (ROW_BLK, 128)
    dma = pltpu.SemaphoreType.DMA
    recv, recv2, slots, flag, pot, table = pl.pallas_call(
        main_kernel,
        name="collocate_exchange",
        out_shape=(
            jax.ShapeDtypeStruct((OWNERS, *block), BF16),
            jax.ShapeDtypeStruct((N, N, *block), BF16),
            jax.ShapeDtypeStruct((N, 128), jnp.int32),
            jax.ShapeDtypeStruct((1, 1), jnp.int32),
            jax.ShapeDtypeStruct((8, 128), F32),
            jax.ShapeDtypeStruct((G * G, *block), BF16),
        ),
        in_specs=[hbm] * 5,
        out_specs=(hbm, hbm, hbm, vmem, hbm, hbm),
        scratch_shapes=[
            pltpu.VMEM((ROWS, EXT3), BF16),
            pltpu.VMEM((ROWS, EXT3), BF16),
            pltpu.VMEM((PAIRS, 4096), BF16),
            pltpu.VMEM((2, PAIRS), jnp.int32),
            pltpu.VMEM((1, PAIRS), jnp.int32),
            pltpu.VMEM((1, PAIRS), jnp.int32),
            pltpu.VMEM((CODES * ROW_BLK, 128), F32),
            pltpu.VMEM((ROWS, WIDE), BF16),
            pltpu.VMEM((ROWS, WIDE), BF16),
            pltpu.VMEM((EXT, 256), F32),
            pltpu.VMEM((len(DIRS), EXT, 256), F32),
            pltpu.VMEM((EXT, 256), F32),
            pltpu.VMEM((ROWS, WIDE), BF16),
            pltpu.VMEM((G * G, *block), BF16),
            pltpu.VMEM((OWNERS, *block), BF16),
            pltpu.VMEM((N, SECOND, *block), BF16),
            pltpu.VMEM((N, SECOND, *block), BF16),
            pltpu.VMEM((N, N, *block), BF16),
            pltpu.VMEM((2, 128), jnp.int32),
            pltpu.SMEM((2, 128), jnp.int32),
            pltpu.VMEM((N, 2, N, 128), jnp.int32),
            pltpu.VMEM((N, 2, N, 128), jnp.int32),
            pltpu.VMEM((N, N, 128), jnp.int32),
            pltpu.VMEM((N, N, 128), jnp.int32),
            pltpu.VMEM((N, 128), jnp.int32),
            pltpu.VMEM((N, N, 128), jnp.int32),
            pltpu.VMEM((8, 128), F32),
            pltpu.VMEM((N, 128), jnp.int32),
            dma((NCHUNK + 4,)),
            dma((5,)),
        ] + [dma] * 14,
        compiler_params=pltpu.CompilerParams(
            collective_id=1, has_side_effects=True, vmem_limit_bytes=61 << 20
        ),
        cost_estimate=pl.CostEstimate(
            flops=4 * ROWS * ROWS * EXT3, bytes_accessed=6 << 20, transcendentals=2 * EXT3
        ),
    )(
        basis.reshape(ROWS, EXT3), density_blocks, pair_groups,
        owner.reshape(1, PAIRS), owner_slot.reshape(1, PAIRS),
    )
    recv2 = recv2.reshape(OWNERS, *block)
    return lax.cond(
        flag[0, 0] > 0,
        lambda: resend(pair_groups, owner, owner_slot, table, slots, recv, recv2, pot),
        lambda: store(slots, recv, recv2, pot),
    )


def solution(mesh):
    return jax.shard_map(
        per_device,
        mesh=mesh,
        in_specs=(
            P(("gx", "gy", "gz"), None, None),
            P(("gx", "gy", "gz"), None),
            P(None, ("gx", "gy", "gz")),
            P(("gx", "gy", "gz"), None),
            P(("gx", "gy", "gz")),
        ),
        out_specs=(P(("gx", "gy", "gz"), None), P("gx", "gy", "gz")),
        check_vma=False,
    )
```

```python
import functools

import jax
import jax.numpy as jnp
from jax import lax
from jax.experimental import pallas as pl
from jax.experimental.pallas import tpu as pltpu
from jax.sharding import PartitionSpec as P

BASIS = 64
RIM = 4
EXT = 16
EXT3 = 4096
XC_COEF = 0.9847450218426965
GRID_WEIGHT = 0.015625
G = 7
ROWS = G * BASIS
WIDE = 512
N = 8
OWNERS = N * N
PAIRS = 48
CODES = 56
ROW_BLK = 32
MESH = pl.DeviceIdType.MESH
F32 = jnp.float32
BF16 = jnp.bfloat16

CHUNK = 2048
NCHUNK = EXT3 // CHUNK

DIRS = [(a, b, c) for c in (0, 1, -1) for a in (0, 1, -1) for b in (0, 1, -1) if (a, b, c) != (0, 0, 0)]
DIR_ID = {d: n for n, d in enumerate(DIRS)}
OUT_PLANE = [d for d in DIRS if d[2] != 0]
FAR_Z = (2, 3, 4, 5, 6)
PEERS = OWNERS - 1 + len(OUT_PLANE) + len(FAR_Z)
FAR_FIRST = (4, 3, 5, 2, 6, 1, 7, 0)
SECOND = 3
FLAG = 128


def half(step, low, high, whole):
    return whole if step == 0 else (high if step > 0 else low)


def bytes_wait(ref, sem):
    pltpu.make_async_copy(ref, ref, sem).wait()


def main_kernel(
    basis_ref, blocks_ref, groups_ref, owner_ref, slot_ref,
    recv_ref, recv2_ref, slots_out, flag_out, pot_ref, table_ref,
    phi, wgt, blk, gv, ov, sv, a3, mperm, mat, rho, hr, vpot, kb, table, send, z2s, z2r, x2s,
    selv, sels, meta, mz, xs, mx, fl, fr, potv, slotv,
    load_sem, own_sem, halo_send, halo_recv, mz_send, mz_recv, mx_send, mx_recv, blk_send, blk_recv,
    z2_send, z2_recv, x2_send, x2_recv, fl_send, fl_recv,
):
    i = lax.axis_index("gx")
    j = lax.axis_index("gy")
    k = lax.axis_index("gz")
    me = i * N + j

    small = []
    for n, (src, dst) in enumerate(((groups_ref, gv), (owner_ref, ov), (slot_ref, sv), (blocks_ref, blk))):
        copy = pltpu.make_async_copy(src, dst, load_sem.at[NCHUNK + n])
        copy.start()
        small.append(copy)
    loads = []
    for n in range(NCHUNK):
        cols = pl.ds(n * CHUNK, CHUNK)
        copy = pltpu.make_async_copy(basis_ref.at[:, cols], phi.at[:, cols], load_sem.at[n])
        copy.start()
        loads.append(copy)

    barrier = pltpu.get_barrier_semaphore()
    gxs = [lax.rem(i + t, N) for t in range(N)]
    gys = [lax.rem(j + t, N) for t in range(N)]
    gzs = [lax.rem(k + t, N) for t in range(N)]
    peers = [(a % N, b % N, c % N) for a, b, c in OUT_PLANE + [(0, 0, t) for t in FAR_Z]]
    peers += [(a, b, 0) for a in FAR_FIRST for b in (4, 3, 5, 2, 6, 1, 7, 0) if (a, b) != (0, 0)]
    for a, b, c in peers:
        pl.semaphore_signal(
            barrier, inc=1, device_id=(gxs[a], gys[b], gzs[c]), device_id_type=MESH
        )

    lane = lax.broadcasted_iota(jnp.int32, (ROW_BLK, 128), 1)
    low = lane < BASIS
    r64 = lax.broadcasted_iota(jnp.int32, (BASIS, BASIS), 0)
    c64 = lax.broadcasted_iota(jnp.int32, (BASIS, BASIS), 1)
    split_rows = jnp.where(c64 == 2 * (r64 % 32) + r64 // 32, 1.0, 0.0).astype(BF16)
    join_rows = jnp.where(r64 == 2 * (c64 % 32) + c64 // 32, 1.0, 0.0).astype(BF16)

    small[0].wait()
    codes = gv[0:1, :] * G + gv[1:2, :]
    pick = jnp.where(
        lax.broadcasted_iota(jnp.int32, (CODES, PAIRS), 0) == codes, 1.0, 0.0
    ).astype(BF16)
    small[3].wait()
    for n in range(8):
        part = jnp.dot(pick, blk[:, n * 512:(n + 1) * 512], preferred_element_type=F32)
        for q in range(4):
            a3[pl.ds(n * 4 + q, CODES, stride=ROW_BLK), :] = part[:, q * 128:(q + 1) * 128]
    for a in range(G):
        for bp in range(4):
            even = a3[(a * G + 2 * bp) * ROW_BLK:(a * G + 2 * bp + 1) * ROW_BLK, :]
            if 2 * bp + 1 < G:
                odd = a3[(a * G + 2 * bp + 1) * ROW_BLK:(a * G + 2 * bp + 2) * ROW_BLK, :]
            else:
                odd = jnp.zeros((ROW_BLK, 128), F32)
            top = jnp.where(low, even, pltpu.roll(odd, 64, axis=1))
            bottom = jnp.where(low, pltpu.roll(even, 64, axis=1), odd)
            mperm[a * 64:a * 64 + 32, bp * 128:(bp + 1) * 128] = top.astype(BF16)
            mperm[a * 64 + 32:(a + 1) * 64, bp * 128:(bp + 1) * 128] = bottom.astype(BF16)
        mat[a * 64:(a + 1) * 64, :] = jnp.dot(
            join_rows, mperm[a * 64:(a + 1) * 64, :], preferred_element_type=F32
        ).astype(BF16)

    for n in range(NCHUNK):
        loads[n].wait()
        cols = slice(n * CHUNK, (n + 1) * CHUNK)
        part = phi[:, cols]
        image = jnp.dot(mat[:, :ROWS], part, preferred_element_type=F32)
        line = jnp.sum(part.astype(F32) * image, axis=0, keepdims=True)
        for q in range(CHUNK // 256):
            x = n * (CHUNK // 256) + q
            rho[x:x + 1, :] = line[:, q * 256:(q + 1) * 256]

    pl.semaphore_wait(barrier, PEERS)

    for n, (a, b, c) in enumerate(DIRS):
        src = rho.at[half(a, pl.ds(0, 8), pl.ds(8, 8), pl.ds(0, 16)),
                     half(b, pl.ds(0, 128), pl.ds(128, 128), pl.ds(0, 256))]
        dst = hr.at[n, half(-a, pl.ds(0, 8), pl.ds(8, 8), pl.ds(0, 16)),
                    half(-b, pl.ds(0, 128), pl.ds(128, 128), pl.ds(0, 256))]
        pltpu.make_async_remote_copy(
            src_ref=src, dst_ref=dst, send_sem=halo_send, recv_sem=halo_recv,
            device_id=(lax.rem(i + a + N, N), lax.rem(j + b + N, N), lax.rem(k + c + N, N)),
            device_id_type=MESH,
        ).start()

    for copy in small[1:3]:
        copy.wait()
    row = lax.broadcasted_iota(jnp.int32, (PAIRS, PAIRS), 0)
    col = lax.broadcasted_iota(jnp.int32, (PAIRS, PAIRS), 1)

    def upright(line):
        return jnp.sum(jnp.where(row == col, line, 0), axis=1, keepdims=True)

    def count(mask, axis):
        return jnp.sum(jnp.where(mask, 1, 0), axis=axis, keepdims=True)

    own_r = ov[...]
    own_c = upright(own_r)
    code_c = upright(codes)
    grp_r = own_r // N
    grp_c = own_c // N
    same = own_c == own_r
    rank_c = count(same & (col < row), 1)
    rank_r = count(same & (row < col), 0)
    mates = grp_c == grp_r
    idx_c = count(mates & (own_r < own_c) & (rank_r > 0), 1)
    idx_r = count(mates & (own_c < own_r) & (rank_c > 0), 0)
    place_c = rank_c * OWNERS + own_c
    place_r = rank_r * OWNERS + own_r
    wide = lax.broadcasted_iota(jnp.int32, (PAIRS, 128), 1)
    sel1 = jnp.sum(jnp.where(wide == place_c, code_c, 0), axis=0, keepdims=True)
    second_at = jnp.where((rank_c > 0) & (idx_c < SECOND), grp_c * SECOND + idx_c, -1)
    sel2 = jnp.sum(jnp.where(wide == second_at, code_c, 0), axis=0, keepdims=True)
    selv[0:1, :] = sel1
    selv[1:2, :] = sel2
    sel_copy = pltpu.make_async_copy(selv, sels, own_sem.at[0])
    sel_copy.start()
    tall = lax.broadcasted_iota(jnp.int32, (OWNERS, PAIRS), 0)
    first_m = tall == place_r
    second_m = tall + OWNERS == place_r
    first_slot = jnp.sum(jnp.where(first_m, sv[...] + 1, 0), axis=1, keepdims=True) - 1
    second_slot = jnp.sum(jnp.where(second_m, sv[...] + 1, 0), axis=1, keepdims=True) - 1
    second_idx = jnp.sum(jnp.where(second_m, idx_r + 1, 0), axis=1, keepdims=True) - 1
    over = jnp.max(jnp.where((rank_r > 0) & (idx_r >= SECOND), FLAG, 0), axis=1, keepdims=True)
    wide64 = lax.broadcasted_iota(jnp.int32, (OWNERS, 128), 1)
    tile = jnp.where(wide64 < OWNERS, first_slot + over, second_slot)
    index = jnp.broadcast_to(second_idx, (OWNERS, 128))
    for t in range(N):
        meta[t, 0] = tile[t * N:(t + 1) * N]
        meta[t, 1] = index[t * N:(t + 1) * N]

    def send_z(t, carry):
        ti = lax.rem(i + t, N)
        pltpu.make_async_remote_copy(
            src_ref=meta.at[ti], dst_ref=mz.at[i], send_sem=mz_send, recv_sem=mz_recv,
            device_id=(ti, j, k), device_id_type=MESH,
        ).start()
        return carry

    lax.fori_loop(1, N, send_z, 0)
    mz[i] = meta[i]

    bytes_wait(hr.at[0:11], halo_recv)
    zlow = lax.rem(lax.broadcasted_iota(jnp.int32, (8, 128), 1), EXT) < 8
    for hx in range(2):
        for hy in range(2):
            rows = slice(hx * 8, hx * 8 + 8)
            cols = slice(hy * 128, hy * 128 + 128)
            total = rho[rows, cols]
            steps_x = (0, 1 - 2 * hx)
            steps_y = (0, 1 - 2 * hy)
            for a in steps_x:
                for b in steps_y:
                    if (a, b) != (0, 0):
                        total = total + hr[DIR_ID[(a, b, 0)], rows, cols]
            sides = []
            for c in (1, -1):
                side = None
                for a in steps_x:
                    for b in steps_y:
                        term = hr[DIR_ID[(a, b, c)], rows, cols]
                        side = term if side is None else side + term
                sides.append(side)
            total = total + jnp.where(
                zlow, pltpu.roll(sides[0], 120, axis=1), pltpu.roll(sides[1], 8, axis=1)
            )
            cubic = jnp.exp(jnp.log(total * total + 1.0) * (-1.0 / 3.0))
            vpot[rows, cols] = -XC_COEF * total * cubic
    left = vpot[4:12, 0:128]
    right = vpot[4:12, 128:256]
    lane8 = lax.broadcasted_iota(jnp.int32, (8, 128), 1)
    potv[...] = jnp.where(
        lane8 < 64, pltpu.roll(left, 64, axis=1), pltpu.roll(right, 64, axis=1)
    )
    pot_copy = pltpu.make_async_copy(potv, pot_ref, own_sem.at[3])
    pot_copy.start()

    for x in range(EXT):
        cols = slice(x * 256, (x + 1) * 256)
        wgt[:, cols] = (phi[:, cols].astype(F32) * vpot[x:x + 1, :]).astype(BF16)
    ks = lax.dot_general(
        wgt[...], phi[...], (((1,), (1,)), ((), ())), preferred_element_type=F32
    )
    kb[:, 0:ROWS] = (ks * GRID_WEIGHT).astype(BF16)
    kb[:, ROWS:] = jnp.zeros((ROWS, WIDE - ROWS), BF16)
    for a in range(G):
        rows = jnp.dot(split_rows, kb[a * 64:(a + 1) * 64, :], preferred_element_type=F32)
        for bp in range(4):
            top = rows[0:32, bp * 128:(bp + 1) * 128]
            bottom = rows[32:64, bp * 128:(bp + 1) * 128]
            table[a * G + 2 * bp] = jnp.where(low, top, pltpu.roll(bottom, 64, axis=1)).astype(BF16)
            if 2 * bp + 1 < G:
                table[a * G + 2 * bp + 1] = jnp.where(
                    low, pltpu.roll(top, 64, axis=1), bottom
                ).astype(BF16)

    sel_copy.wait()
    keep = pltpu.make_async_copy(table, table_ref, own_sem.at[0])
    keep.start()

    def pack_second(ti):
        for c in range(SECOND):
            z2s[ti, c] = table[sels[1, ti * SECOND + c]]

    for di in FAR_FIRST[:-1]:
        ti = lax.rem(i + di, N)
        pack_second(ti)
        pltpu.make_async_remote_copy(
            src_ref=z2s.at[ti], dst_ref=z2r.at[i], send_sem=z2_send, recv_sem=z2_recv,
            device_id=(ti, j, k), device_id_type=MESH,
        ).start()
    pack_second(i)
    z2r[i] = z2s[i]

    bytes_wait(mz.at[0:N - 1], mz_recv)
    for t in range(N):
        xs[t] = mz[:, 0, t, :]

    def send_x(t, carry):
        tj = lax.rem(j + t, N)
        pltpu.make_async_remote_copy(
            src_ref=xs.at[tj], dst_ref=mx.at[j], send_sem=mx_send, recv_sem=mx_recv,
            device_id=(i, tj, k), device_id_type=MESH,
        ).start()
        return carry

    lax.fori_loop(1, N, send_x, 0)
    mx[j] = xs[j]

    for di in FAR_FIRST:
        ti = lax.rem(i + di, N)

        def send_block(t, carry, ti=ti):
            tj = lax.rem(j + t, N)
            target = ti * N + tj
            send[target] = table[sels[0, target]]
            pltpu.make_async_remote_copy(
                src_ref=send.at[target], dst_ref=recv_ref.at[me], send_sem=blk_send,
                recv_sem=blk_recv, device_id=(ti, tj, k), device_id_type=MESH,
            ).start()
            return carry

        lax.fori_loop(0 if di else 1, N, send_block, 0)
    send[me] = table[sels[0, me]]
    own = pltpu.make_async_copy(send.at[me], recv_ref.at[me], own_sem.at[1])
    own.start()

    bytes_wait(mx.at[0:N - 1], mx_recv)
    wide8 = lax.broadcasted_iota(jnp.int32, (N, 128), 1)
    sub8 = lax.broadcasted_iota(jnp.int32, (N, 128), 0)
    slots = jnp.zeros((N, 128), jnp.int32)
    over = jnp.zeros((N, 128), jnp.int32)
    for t in range(N):
        part = mx[t]
        left_over = (wide8 < OWNERS) & (part >= FLAG - 1)
        over = jnp.maximum(over, jnp.where(left_over, 1, 0))
        value = jnp.where(left_over, part - FLAG, part)
        here = (wide8 == sub8 * N + t) | (wide8 == OWNERS + t * N + sub8)
        slots = slots + jnp.where(here, value, 0)
    slotv[...] = jnp.broadcast_to(jnp.sum(slots, axis=0, keepdims=True), (N, 128))
    slot_copy = pltpu.make_async_copy(slotv, slots_out, own_sem.at[4])
    slot_copy.start()
    fl[...] = over

    def send_flag(t, carry):
        tk = lax.rem(k + t, N)
        pltpu.make_async_remote_copy(
            src_ref=fl, dst_ref=fr.at[k], send_sem=fl_send, recv_sem=fl_recv,
            device_id=(i, j, tk), device_id_type=MESH,
        ).start()
        return carry

    lax.fori_loop(1, N, send_flag, 0)
    fr[k] = over

    bytes_wait(z2r.at[0:N - 1], z2_recv)
    for dj in FAR_FIRST:
        tj = lax.rem(j + dj, N)

        def place_second(a, carry, tj=tj):
            index = jnp.broadcast_to(mz[a, 1, pl.ds(tj, 1), :], (ROW_BLK, 128))
            total = jnp.zeros((ROW_BLK, 128), F32)
            for c in range(SECOND):
                total = jnp.where(index == c, z2r[a, c].astype(F32), total)
            x2s[tj, a] = total.astype(BF16)
            return carry

        lax.fori_loop(0, N, place_second, 0)
        if dj:
            pltpu.make_async_remote_copy(
                src_ref=x2s.at[tj], dst_ref=recv2_ref.at[j], send_sem=x2_send, recv_sem=x2_recv,
                device_id=(i, tj, k), device_id_type=MESH,
            ).start()
    own2 = pltpu.make_async_copy(x2s.at[j], recv2_ref.at[j], own_sem.at[2])
    own2.start()

    bytes_wait(fr.at[0:N - 1], fl_recv)
    for t in range(N):
        over = jnp.maximum(over, fr[t])
    flag_out[...] = jnp.max(jnp.max(over, axis=0, keepdims=True), axis=1, keepdims=True)

    for copy in (keep, pot_copy, slot_copy):
        copy.wait()
    own.wait()
    own2.wait()
    bytes_wait(fr.at[0:N - 1], fl_send)
    bytes_wait(xs.at[0:N - 1], mx_send)
    bytes_wait(mz.at[0:N - 1], mz_send)
    bytes_wait(hr.at[0:11], halo_send)
    bytes_wait(z2s.at[0:N - 1], z2_send)
    bytes_wait(x2s.at[0:N - 1], x2_send)
    bytes_wait(send.at[0:OWNERS - 1], blk_send)
    bytes_wait(recv2_ref.at[0:N - 1], x2_recv)
    bytes_wait(recv_ref.at[0:OWNERS - 1], blk_recv)


def store_kernel(slots_ref, recv_ref, recv2_ref, pot_ref, out_ref, pot_out, acc):
    acc[...] = jnp.zeros_like(acc)
    pot = pot_ref[...]
    for y in range(8):
        pot_out[:, y, :] = pot[:, y * EXT + RIM:y * EXT + RIM + 8]

    def add(t, carry):
        for rank, ref in enumerate((recv_ref, recv2_ref)):
            slot = slots_ref[0, rank * OWNERS + t]
            slot = jnp.where(slot < 0, PAIRS, slot)
            at = pl.ds(pl.multiple_of(slot * ROW_BLK, ROW_BLK), ROW_BLK)
            acc[at, :] += ref[t].astype(F32)
        return carry

    lax.fori_loop(0, OWNERS, add, 0, unroll=4)
    for c in range(ROW_BLK):
        out_ref[:, c * 128:(c + 1) * 128] = acc[pl.ds(c, PAIRS, stride=ROW_BLK), :].astype(BF16)


def store(slots, recv, recv2, pot):
    vmem = pl.BlockSpec(memory_space=pltpu.VMEM)
    smem = pl.BlockSpec(memory_space=pltpu.SMEM)
    return pl.pallas_call(
        store_kernel,
        name="store_blocks",
        out_shape=(
            jax.ShapeDtypeStruct((PAIRS, 4096), BF16),
            jax.ShapeDtypeStruct((8, 8, 8), F32),
        ),
        in_specs=[smem, vmem, vmem, vmem],
        out_specs=(vmem, vmem),
        scratch_shapes=[pltpu.VMEM(((PAIRS + 1) * ROW_BLK, 128), F32)],
        compiler_params=pltpu.CompilerParams(vmem_limit_bytes=16 << 20),
    )(slots, recv, recv2, pot)


def resend(pair_groups, owner, owner_slot, table, slots, recv, recv2, pot):
    codes = pair_groups[0] * G + pair_groups[1]
    names = owner[:, 0]
    order = jnp.arange(PAIRS, dtype=jnp.int32)
    earlier = (names[:, None] == names[None, :]) & (order[:, None] > order[None, :])
    rank = jnp.sum(earlier.astype(jnp.int32), axis=1)
    match = (jnp.arange(OWNERS, dtype=jnp.int32)[:, None] == names[None, :]) & (rank[None, :] == 1)
    pick = jnp.sum(jnp.where(match, codes[None, :], 0), axis=1)
    second = jnp.sum(jnp.where(match, owner_slot[None, :] + 1, 0), axis=1) - 1
    chosen = (jnp.arange(G * G, dtype=jnp.int32)[None, :] == pick[:, None]).astype(BF16)
    blocks = lax.dot_general(
        chosen, table, (((1,), (0,)), ((), ())), preferred_element_type=F32
    ).astype(BF16)
    got = lax.all_to_all(blocks, ("gx", "gy"), split_axis=0, concat_axis=0, tiled=True)
    got_slots = lax.all_to_all(second, ("gx", "gy"), split_axis=0, concat_axis=0, tiled=True)
    new = jnp.concatenate([slots[:, :OWNERS], jnp.broadcast_to(got_slots[None], (N, OWNERS))], axis=1)
    return store(new, recv, got, pot)


def per_device(basis, density_blocks, pair_groups, owner, owner_slot):
    vmem = pl.BlockSpec(memory_space=pltpu.VMEM)
    hbm = pl.BlockSpec(memory_space=pl.ANY)
    block = (ROW_BLK, 128)
    dma = pltpu.SemaphoreType.DMA
    recv, recv2, slots, flag, pot, table = pl.pallas_call(
        main_kernel,
        name="collocate_exchange",
        out_shape=(
            jax.ShapeDtypeStruct((OWNERS, *block), BF16),
            jax.ShapeDtypeStruct((N, N, *block), BF16),
            jax.ShapeDtypeStruct((N, 128), jnp.int32),
            jax.ShapeDtypeStruct((1, 1), jnp.int32),
            jax.ShapeDtypeStruct((8, 128), F32),
            jax.ShapeDtypeStruct((G * G, *block), BF16),
        ),
        in_specs=[hbm] * 5,
        out_specs=(hbm, hbm, hbm, vmem, hbm, hbm),
        scratch_shapes=[
            pltpu.VMEM((ROWS, EXT3), BF16),
            pltpu.VMEM((ROWS, EXT3), BF16),
            pltpu.VMEM((PAIRS, 4096), BF16),
            pltpu.VMEM((2, PAIRS), jnp.int32),
            pltpu.VMEM((1, PAIRS), jnp.int32),
            pltpu.VMEM((1, PAIRS), jnp.int32),
            pltpu.VMEM((CODES * ROW_BLK, 128), F32),
            pltpu.VMEM((ROWS, WIDE), BF16),
            pltpu.VMEM((ROWS, WIDE), BF16),
            pltpu.VMEM((EXT, 256), F32),
            pltpu.VMEM((len(DIRS), EXT, 256), F32),
            pltpu.VMEM((EXT, 256), F32),
            pltpu.VMEM((ROWS, WIDE), BF16),
            pltpu.VMEM((G * G, *block), BF16),
            pltpu.VMEM((OWNERS, *block), BF16),
            pltpu.VMEM((N, SECOND, *block), BF16),
            pltpu.VMEM((N, SECOND, *block), BF16),
            pltpu.VMEM((N, N, *block), BF16),
            pltpu.VMEM((2, 128), jnp.int32),
            pltpu.SMEM((2, 128), jnp.int32),
            pltpu.VMEM((N, 2, N, 128), jnp.int32),
            pltpu.VMEM((N, 2, N, 128), jnp.int32),
            pltpu.VMEM((N, N, 128), jnp.int32),
            pltpu.VMEM((N, N, 128), jnp.int32),
            pltpu.VMEM((N, 128), jnp.int32),
            pltpu.VMEM((N, N, 128), jnp.int32),
            pltpu.VMEM((8, 128), F32),
            pltpu.VMEM((N, 128), jnp.int32),
            dma((NCHUNK + 4,)),
            dma((5,)),
        ] + [dma] * 14,
        compiler_params=pltpu.CompilerParams(
            collective_id=1, has_side_effects=True, vmem_limit_bytes=61 << 20
        ),
        cost_estimate=pl.CostEstimate(
            flops=4 * ROWS * ROWS * EXT3, bytes_accessed=6 << 20, transcendentals=2 * EXT3
        ),
    )(
        basis.reshape(ROWS, EXT3), density_blocks, pair_groups,
        owner.reshape(1, PAIRS), owner_slot.reshape(1, PAIRS),
    )
    recv2 = recv2.reshape(OWNERS, *block)
    return lax.cond(
        flag[0, 0] > 0,
        lambda: resend(pair_groups, owner, owner_slot, table, slots, recv, recv2, pot),
        lambda: store(slots, recv, recv2, pot),
    )


def solution(mesh):
    return jax.shard_map(
        per_device,
        mesh=mesh,
        in_specs=(
            P(("gx", "gy", "gz"), None, None),
            P(("gx", "gy", "gz"), None),
            P(None, ("gx", "gy", "gz")),
            P(("gx", "gy", "gz"), None),
            P(("gx", "gy", "gz")),
        ),
        out_specs=(P(("gx", "gy", "gz"), None), P("gx", "gy", "gz")),
        check_vma=False,
    )
```
